256 devices in a mesh: src: 32 (over z_hi, x, core), tgt: 8 (over y, z_lo).
Axes of the slice: x: 4, y: 4, z: 8 (z_hi: 4, z_lo: 2; z = z_hi * 2 + z_lo), core: 2. Of those that a mesh axis runs over, the one named last changes fastest.
Arguments:
- source_feats: bfloat16 [32, 512, 384], P('src', 'tgt'), may hold values from -64 to 64
- source_tiles: bfloat16 [32, 512, 128], P('src', 'tgt'), may hold values from -0.5 to 0.5
- source_links: int32 [32, 8, 2], P('src', 'tgt'), may hold values from 0 to 7, as said below
- target_feats: bfloat16 [8, 2048, 384], P('tgt', 'src'), may hold values from -64 to 64
- target_tiles: bfloat16 [8, 2048, 128], P('tgt', 'src'), may hold values from -0.5 to 0.5
- target_links: int32 [8, 32, 2], P('tgt', 'src'), may hold values from 0 to 31, as said below
- near_first: bfloat16 [384, 384], replicated, may hold values from -0.3125 to 0.3125
- self_first: bfloat16 [384, 384], replicated, may hold values from -0.3125 to 0.3125
- near_second: bfloat16 [384, 384], replicated, may hold values from -0.3125 to 0.3125
- self_second: bfloat16 [384, 384], replicated, may hold values from -0.3125 to 0.3125
Outputs:
- source_potential: float32 [16384], P('src')
- target_potential: float32 [16384], P('tgt')
The draws below stay inside these ranges and needn't reach their ends.
Inputs may be any that keep to these rules, and one draw needn't show every extreme that they name: `source_links`: the first entry of partition p is 7 - p; the other entries may repeat. `target_links`: the first entry of partition q is 31 - q; the other entries may repeat.
All inputs are finite; a program needn't handle non-finite values.
Results may differ from the reference program's by a relative error of at most 0.0036.
Values may be sent and summed in bfloat16 or wider, within the bound.
No kernel may reach another device: no remote copies, remote signals or barrier semaphores. Data moves between devices by JAX's collectives and lax.ppermute only.
A program may use at most 64 MiB of HBM per device.

```python
import math
import jax
import jax.numpy as jnp
from jax import lax

D = 384
K_NB = 2
S_DEV = 512
T_DEV = 2048
SE = 64
TE = 64
NS = 16384
NT = 16384
N_SRC = 32
N_TGT = 8


def draw_source_feats(key, part):
    key = jax.random.fold_in(key, 3)
    value_key = jax.random.fold_in(key, 0)
    full_shape = (N_SRC, S_DEV, D)
    values = jnp.clip(jax.random.normal(value_key, full_shape, jnp.float32), -6.0, 6.0)
    return values.astype(jnp.bfloat16)


def draw_target_feats(key, part):
    key = jax.random.fold_in(key, 5)
    value_key = jax.random.fold_in(key, 0)
    full_shape = (N_TGT, T_DEV, D)
    values = jnp.clip(jax.random.normal(value_key, full_shape, jnp.float32), -6.0, 6.0)
    return values.astype(jnp.bfloat16)


def neighbour_lists(key, groups, count):
    order_key = jnp.arange(count, dtype=jnp.int32)
    first_entry = jnp.broadcast_to((count - 1 - order_key)[None, :, None], (groups, count, 1))
    later_entries = jax.random.randint(key, (groups, count, K_NB - 1), 0, count)
    return jnp.concatenate([first_entry.astype(jnp.int32), later_entries.astype(jnp.int32)], axis=-1)


def draw_source_links(key, part):
    key = jax.random.fold_in(key, 7)
    return neighbour_lists(key, N_SRC, N_TGT)


def draw_target_links(key, part):
    key = jax.random.fold_in(key, 11)
    return neighbour_lists(key, N_TGT, N_SRC)


def levels(key, extent, cuts, least, largest):
    level, own = 1.0, jax.random.fold_in(key, 6)
    for axis_at, blocks in cuts:
        draws = jnp.exp(jax.random.uniform(jax.random.fold_in(own, axis_at), (blocks,), jnp.float32, least / len(cuts), largest / len(cuts)))
        level = level * jnp.repeat(draws, extent[axis_at] // blocks).reshape([-1 if axis == axis_at else 1 for axis in range(len(extent))])
    return level


def bell_draw(key, dims, deviation, most, cuts=(), held_as=jnp.bfloat16):
    result = deviation * jax.random.normal(key, dims, jnp.float32)
    if cuts:
        result = result * levels(key, dims, cuts, -0.22, 0.18)
    return jnp.clip(result, -most, most).astype(held_as)


def setup_inputs(seed: int = 0) -> dict:
    key_list = jax.random.split(jax.random.key(seed), 11)
    return {
        "source_feats": draw_source_feats(jax.random.fold_in(key_list[10], 71), 0),
        "source_tiles": bell_draw(key_list[1], (N_SRC, S_DEV, K_NB * SE), (K_NB * SE) ** -0.5, 0.5, ((0, 32), (1, 8))),
        "source_links": draw_source_links(jax.random.fold_in(key_list[10], 71), 0),
        "target_feats": draw_target_feats(jax.random.fold_in(key_list[10], 71), 0),
        "target_tiles": bell_draw(key_list[4], (N_TGT, T_DEV, K_NB * TE), (K_NB * TE) ** -0.5, 0.5, ((0, 8), (1, 32))),
        "target_links": draw_target_links(jax.random.fold_in(key_list[10], 71), 0),
        "near_first": bell_draw(key_list[6], (D, D), D ** -0.5, 0.3125),
        "self_first": bell_draw(key_list[7], (D, D), D ** -0.5, 0.3125),
        "near_second": bell_draw(key_list[8], (D, D), D ** -0.5, 0.3125),
        "self_second": bell_draw(key_list[9], (D, D), D ** -0.5, 0.3125),
    }


def neighbour_sum(hidden, panels, links, row_count):
    def one_group(items):
        group_rows, group_panel, group_links = items
        blocks = group_rows.reshape(-1, row_count, D)
        picked = blocks[group_links].astype(jnp.float32)
        shaped = group_panel.reshape(-1, row_count, K_NB, row_count).astype(jnp.float32)
        return jnp.einsum('prkc,pkcd->prd', shaped, picked).reshape(-1, D)
    return lax.map(one_group, (hidden, panels, links)).astype(jnp.bfloat16)


def embed(features, panels, links, row_count, weights):
    hidden = features
    for layer_index in range(2):
        summed = neighbour_sum(hidden, panels, links, row_count)
        mixed = jnp.dot(summed.reshape(-1, D), weights[2 * layer_index], preferred_element_type=jnp.float32)
        mixed = mixed + jnp.dot(hidden.reshape(-1, D), weights[2 * layer_index + 1], preferred_element_type=jnp.float32)
        if layer_index == 0:
            mixed = jax.nn.relu(mixed)
        hidden = mixed.astype(jnp.bfloat16).reshape(features.shape)
    return hidden.reshape(-1, D)


def reference(source_feats, source_tiles, source_links, target_feats, target_tiles, target_links, near_first, self_first, near_second, self_second):
    weights = (near_first, self_first, near_second, self_second)
    emb_source = embed(source_feats, source_tiles, source_links, SE, weights)
    emb_target = embed(target_feats, target_tiles, target_links, TE, weights)
    block_size = math.gcd(NS, 1024)
    row_blocks = emb_source.reshape(NS // block_size, block_size, D)

    def logits(row_block):
        return 0.2 * jnp.dot(row_block, emb_target.T, preferred_element_type=jnp.float32)

    target_potential = jnp.zeros((NT,), jnp.float32)
    source_potential = jnp.zeros((NS,), jnp.float32)
    for sweep_index in range(2):
        def row_pass(row_block):
            shifted = logits(row_block) + target_potential[None, :]
            top = jnp.max(shifted, axis=1)
            return top + jnp.log(jnp.sum(jnp.exp(shifted - top[:, None]), axis=1))

        source_potential = math.log(NT) - lax.map(row_pass, row_blocks).reshape(NS)
        potential_blocks = source_potential.reshape(NS // block_size, block_size)

        def col_pass(carry, items):
            top, total = carry
            row_block, block_potential = items
            shifted = logits(row_block) + block_potential[:, None]
            new_top = jnp.maximum(top, jnp.max(shifted, axis=0))
            total = total * jnp.exp(top - new_top) + jnp.sum(jnp.exp(shifted - new_top[None, :]), axis=0)
            return (new_top, total), None

        start = (jnp.full((NT,), -jnp.inf, jnp.float32), jnp.zeros((NT,), jnp.float32))
        (top, total), _ = lax.scan(col_pass, start, (row_blocks, potential_blocks))
        target_potential = math.log(NS) - (top + jnp.log(total))
    return source_potential, target_potential
```

```python
import functools
import math

import jax
import jax.numpy as jnp
from jax import lax
from jax.experimental import pallas as pl
from jax.experimental.pallas import tpu as pltpu
from jax.sharding import Mesh, PartitionSpec as P

D = 384
PART = 64
PACK = 272
ROWS = 512
COLS = 2048
LANES = 128
ROW_BLOCKS = ROWS // LANES
COL_BLOCKS = COLS // LANES
N_TGT = 8
N_PEERS = 16
LOG_N = math.log(16384.0)
VMEM_LIMIT = 32 * 1024 * 1024

VMEM = functools.partial(pl.BlockSpec, memory_space=pltpu.VMEM)
SMEM = functools.partial(pl.BlockSpec, memory_space=pltpu.SMEM)


def pack(features, tiles, links):
    link = jnp.broadcast_to(links[0, 0, 1].astype(jnp.bfloat16), (16, LANES))
    feats = features[0]
    pieces = [feats[:, at : at + LANES] for at in range(0, D, LANES)]
    return jnp.concatenate(pieces + [tiles[0], link], axis=0)[None]


def graph_layers(packed, first, second, near1, self1, near2, self2, x_ref, s_ref, h_ref, emit):
    count = x_ref.shape[0] // PART
    for k in range(count):
        ref, at = packed(k)
        for piece in range(D // LANES):
            x_ref[k * PART : (k + 1) * PART, piece * LANES : (piece + 1) * LANES] = ref[
                at, piece * PART : (piece + 1) * PART, :
            ]

    def neighbour_sums(src):
        for k in range(count):
            ref, at = packed(k)
            near = src[pl.ds(first(k) * PART, PART), :]
            other = src[pl.ds(pl.multiple_of(second(k) * PART, PART), PART), :]
            panel = ref[at, 3 * PART : 4 * PART, :]
            both = jnp.concatenate([near, other], axis=0)
            total = jnp.dot(panel, both, preferred_element_type=jnp.float32)
            s_ref[k * PART : (k + 1) * PART, :] = total.astype(jnp.bfloat16)

    step = 256
    neighbour_sums(x_ref)
    for at in range(0, count * PART, step):
        rows = pl.ds(at, step)
        mixed = jnp.dot(s_ref[rows, :], near1[...], preferred_element_type=jnp.float32)
        mixed += jnp.dot(x_ref[rows, :], self1[...], preferred_element_type=jnp.float32)
        h_ref[rows, :] = jnp.maximum(mixed, 0.0).astype(jnp.bfloat16)
    neighbour_sums(h_ref)
    for at in range(0, count * PART, step):
        rows = pl.ds(at, step)
        mixed = jnp.dot(s_ref[rows, :], near2[...], preferred_element_type=jnp.float32)
        mixed += jnp.dot(h_ref[rows, :], self2[...], preferred_element_type=jnp.float32)
        emit(at, mixed.astype(jnp.bfloat16))


def source_kernel(links, packed, near1, self1, near2, self2, out, x_ref, s_ref, h_ref):
    def emit(at, value):
        out[at : at + value.shape[0], :] = value

    graph_layers(
        lambda k: (packed, k),
        lambda k: 7 - k,
        lambda k: links[k],
        near1, self1, near2, self2, x_ref, s_ref, h_ref, emit,
    )


def slot_xor(k):
    b0, b1, b2, b3, b4 = ((k >> bit) & 1 for bit in range(5))
    return ((b0 ^ (3 * b1)) << 3) | ((b2 ^ (3 * b3)) << 1) | b4


SLOT_OF = {slot_xor(k): k for k in range(32)}


def slot_of(v):
    z1, z0, x1, x0, c = ((v >> bit) & 1 for bit in (4, 3, 2, 1, 0))
    return (z0 ^ z1) | (z1 << 1) | ((x0 ^ x1) << 2) | (x1 << 3) | (c << 4)


def spread(row):
    return jnp.transpose(jnp.broadcast_to(row, (LANES, LANES)))


def target_kernel(
    links, own, other, near1, self1, near2, self2, emb_source,
    scores, send,
    x_ref, s_ref, h_ref, e_ref,
):
    me = links[32]

    def emit(at, value):
        for piece in range(value.shape[0] // PART):
            q = me ^ slot_xor(at // PART + piece)
            e_ref[pl.ds(pl.multiple_of(q * PART, PART), PART), :] = value[piece * PART : (piece + 1) * PART, :]

    graph_layers(
        lambda k: (own, k) if k < 16 else (other, k - 16),
        lambda k: k ^ SLOT_OF[31],
        lambda k: links[k],
        near1, self1, near2, self2, x_ref, s_ref, h_ref, emit,
    )

    for i in range(COL_BLOCKS // 2):
        part = lax.dot_general(
            emb_source[...],
            e_ref[i * 256 : (i + 1) * 256, :],
            (((1,), (1,)), ((), ())),
            preferred_element_type=jnp.float32,
        )
        part = 0.2 * part
        scores[2 * i] = part[:, :LANES]
        scores[2 * i + 1] = part[:, LANES:]

    for b in range(ROW_BLOCKS):
        rows = pl.ds(b * LANES, LANES)
        top = scores[0, rows, :]
        for i in range(1, COL_BLOCKS):
            top = jnp.maximum(top, scores[i, rows, :])
        total = jnp.exp(scores[0, rows, :] - top)
        for i in range(1, COL_BLOCKS):
            total += jnp.exp(scores[i, rows, :] - top)
        top, total = jnp.transpose(top), jnp.transpose(total)
        larger = jnp.max(top, axis=0, keepdims=True)
        total = jnp.sum(total * jnp.exp(top - larger), axis=0, keepdims=True)
        for d in range(N_TGT):
            send[d, b : b + 1, :] = larger
            send[d, b + 4 : b + 5, :] = total


def column_kernel(scores, got, weights, tops, lse, potential, shift):
    top, total = got[0, 0:4, :], got[0, 4:8, :]
    larger = top
    for d in range(1, N_TGT):
        larger = jnp.maximum(larger, got[d, 0:4, :])
    total = total * jnp.exp(top - larger)
    for d in range(1, N_TGT):
        total += got[d, 4:8, :] * jnp.exp(got[d, 0:4, :] - larger)
    source = LOG_N - (larger + jnp.log(total))
    potential[0:4, :] = source
    potential[4:8, :] = source
    for b in range(ROW_BLOCKS):
        shift[pl.ds(b * LANES, LANES), :] = spread(source[b : b + 1, :])

    @pl.loop(0, COL_BLOCKS)
    def _(i):
        x = (scores[i] + shift[...]).reshape(ROWS // 8, 8, LANES)
        top = jnp.max(x, axis=0)
        e = jnp.exp(x - top[None])
        weights[i] = e.reshape(ROWS, LANES)
        total = jnp.sum(e, axis=0)
        tops[i] = top
        larger = jnp.max(top, axis=0, keepdims=True)
        total = jnp.sum(total * jnp.exp(top - larger), axis=0, keepdims=True)
        lse[pl.ds(i, 1), :] = larger + jnp.log(total)


def row_kernel(weights, tops, got, send, potential, scale):
    larger = got[0]
    for d in range(1, N_PEERS):
        larger = jnp.maximum(larger, got[d])
    total = jnp.exp(got[0] - larger)
    for d in range(1, N_PEERS):
        total += jnp.exp(got[d] - larger)
    target = LOG_N - (larger + jnp.log(total))
    potential[...] = target
    for i in range(COL_BLOCKS):
        scale[i] = jnp.exp(tops[i] + target[i : i + 1, :])
    for b in range(ROW_BLOCKS):
        rows = pl.ds(b * LANES, LANES)
        total = jnp.zeros((LANES // 8, 8, LANES), jnp.float32)
        for i in range(COL_BLOCKS):
            total += weights[i, rows, :].reshape(LANES // 8, 8, LANES) * scale[i][None]
        total = jnp.transpose(total.reshape(LANES, LANES))
        total = jnp.sum(total, axis=0, keepdims=True)
        for d in range(N_TGT):
            send[d, b : b + 1, :] = total
            send[d, b + 4 : b + 5, :] = total


def last_kernel(weights, scale, got, before, sums, potential, factor):
    total = got[0, 0:4, :]
    for d in range(1, N_TGT):
        total += got[d, 0:4, :]
    source = before[0:4, :] + (LOG_N - jnp.log(total))
    potential[0:4, :] = source
    potential[4:8, :] = source
    ratio = 16384.0 / total
    for b in range(ROW_BLOCKS):
        factor[pl.ds(b * LANES, LANES), :] = spread(ratio[b : b + 1, :])

    @pl.loop(0, COL_BLOCKS)
    def _(i):
        e = (weights[i] * factor[...]).reshape(ROWS // 8, 8, LANES)
        sums[pl.ds(i, 1), :] = jnp.sum(jnp.sum(e, axis=0) * scale[i], axis=0, keepdims=True)


def call(kernel, outs, scratch, ins):
    return pl.pallas_call(
        kernel,
        out_shape=[jax.ShapeDtypeStruct(shape, dtype) for shape, dtype in outs],
        in_specs=ins,
        out_specs=[VMEM() for _ in outs],
        scratch_shapes=scratch,
        compiler_params=pltpu.CompilerParams(vmem_limit_bytes=VMEM_LIMIT),
    )


def swap(value, axis, size, xor):
    return lax.ppermute(value, axis, [(i, i ^ xor) for i in range(size)])


def exchange(value, axes):
    return lax.all_to_all(value, axes, 0, 0)


def on_device(
    source_feats, source_tiles, source_links, target_feats, target_tiles, target_links,
    near_first, self_first, near_second, self_second,
):
    f32, bf16 = jnp.float32, jnp.bfloat16
    weights = (near_first, self_first, near_second, self_second)
    me = lax.axis_index(("zh", "x", "c"))

    held = pack(target_feats, target_tiles, target_links)
    for axis, xor in (("zh", 1), ("zh", 3), ("x", 1), ("x", 3)):
        held = jnp.concatenate([held, swap(held, axis, 4, xor)], axis=0)
    other = swap(held, "c", 2, 1)

    packed = pack(source_feats, source_tiles, source_links)
    packed = exchange(jnp.broadcast_to(packed, (N_TGT, PACK, LANES)), ("y", "zl"))
    source_second = packed[:, 4 * PART, 0].astype(jnp.int32)
    (emb_source,) = call(
        source_kernel,
        [((ROWS, D), bf16)],
        [pltpu.VMEM((ROWS, D), bf16)] * 3,
        [SMEM()] + [VMEM()] * 5,
    )(source_second, packed, *weights)

    target_second = jnp.concatenate([held[:, 4 * PART, 0], other[:, 4 * PART, 0]]).astype(jnp.int32)
    target_slots = jnp.concatenate([slot_of(target_second ^ me), me[None]])
    scores, send = call(
        target_kernel,
        [((COL_BLOCKS, ROWS, LANES), f32), ((N_TGT, 8, LANES), f32)],
        [pltpu.VMEM((COLS, D), bf16)] * 4,
        [SMEM()] + [VMEM()] * 7,
    )(target_slots, held, other, *weights, emb_source)

    got = exchange(send, ("y", "zl"))
    spread_weights, tops, lse, source_first = call(
        column_kernel,
        [
            ((COL_BLOCKS, ROWS, LANES), f32),
            ((COL_BLOCKS, 8, LANES), f32),
            ((COL_BLOCKS, LANES), f32),
            ((8, LANES), f32),
        ],
        [pltpu.VMEM((ROWS, LANES), f32)],
        [VMEM()] * 2,
    )(scores, got)

    lse = jnp.logaddexp(lse, swap(lse, "c", 2, 1))
    got = exchange(jnp.broadcast_to(lse, (N_PEERS, COL_BLOCKS, LANES)), ("zh", "x"))
    send, target_first, scale = call(
        row_kernel,
        [((N_TGT, 8, LANES), f32), ((COL_BLOCKS, LANES), f32), ((COL_BLOCKS, 8, LANES), f32)],
        [],
        [VMEM()] * 3,
    )(spread_weights, tops, got)

    got = exchange(send, ("y", "zl"))
    sums, source_potential = call(
        last_kernel,
        [((COL_BLOCKS, LANES), f32), ((8, LANES), f32)],
        [pltpu.VMEM((ROWS, LANES), f32)],
        [VMEM()] * 4,
    )(spread_weights, scale, got, source_first)

    sums = sums + swap(sums, "c", 2, 1)
    got = exchange(jnp.broadcast_to(sums, (N_PEERS, COL_BLOCKS, LANES)), ("zh", "x"))
    target_potential = target_first + (LOG_N - jnp.log(jnp.sum(got, axis=0)))
    return source_potential[0:4].reshape(ROWS), target_potential.reshape(COLS)


def solution(mesh):
    fine = Mesh(mesh.devices.reshape(4, 4, 2, 4, 2), ("zh", "x", "c", "y", "zl"))
    src, tgt = ("zh", "x", "c"), ("y", "zl")
    return jax.shard_map(
        on_device,
        mesh=fine,
        in_specs=(P(src, tgt, None),) * 3 + (P(tgt, src, None),) * 3 + (P(),) * 4,
        out_specs=(P(src), P(tgt)),
        check_vma=False,
    )
```

```python
import functools
import math

import jax
import jax.numpy as jnp
from jax import lax
from jax.experimental import pallas as pl
from jax.experimental.pallas import tpu as pltpu
from jax.sharding import Mesh, PartitionSpec as P

D = 384
PART = 64
PACK = 272
ROWS = 512
COLS = 2048
LANES = 128
ROW_BLOCKS = ROWS // LANES
COL_BLOCKS = COLS // LANES
N_TGT = 8
STEP = 512
N_PEERS = 16
LOG_N = math.log(16384.0)
VMEM_LIMIT = 32 * 1024 * 1024

VMEM = functools.partial(pl.BlockSpec, memory_space=pltpu.VMEM)
SMEM = functools.partial(pl.BlockSpec, memory_space=pltpu.SMEM)


def pack_kernel(t_links, s_links, t_feats, t_tiles, s_feats, s_tiles, held, packed):
    def put(ref, at, feats, tiles, link):
        for piece in range(D // LANES):
            ref[at, piece * PART : (piece + 1) * PART, :] = feats[0, :, piece * LANES : (piece + 1) * LANES]
        ref[at, 3 * PART : 4 * PART, :] = tiles[0]
        ref[at, 4 * PART : PACK, :] = jnp.full((16, LANES), link.astype(jnp.float32)).astype(jnp.bfloat16)

    put(held, 0, t_feats, t_tiles, t_links[0, 0, 1])
    for d in range(N_TGT):
        put(packed, d, s_feats, s_tiles, s_links[0, 0, 1])


def graph_layers(packed, first, second, near1, self1, near2, self2, x_ref, s_ref, h_ref, emit):
    count = x_ref.shape[0] // PART
    for k in range(count):
        ref, at = packed(k)
        for piece in range(D // LANES):
            x_ref[k * PART : (k + 1) * PART, piece * LANES : (piece + 1) * LANES] = ref[
                at, piece * PART : (piece + 1) * PART, :
            ]

    def neighbour_sums(src):
        for k in range(count):
            ref, at = packed(k)
            near = src[pl.ds(first(k) * PART, PART), :]
            other = src[pl.ds(pl.multiple_of(second(k) * PART, PART), PART), :]
            panel = ref[at, 3 * PART : 4 * PART, :]
            both = jnp.concatenate([near, other], axis=0)
            total = jnp.dot(panel, both, preferred_element_type=jnp.float32)
            s_ref[k * PART : (k + 1) * PART, :] = total.astype(jnp.bfloat16)

    def mix(src, at, near, own):
        left = jnp.concatenate([s_ref[at : at + STEP, :], src[at : at + STEP, :]], axis=1)
        right = jnp.concatenate([near[...], own[...]], axis=0)
        return jnp.dot(left, right, preferred_element_type=jnp.float32)

    neighbour_sums(x_ref)
    for at in range(0, count * PART, STEP):
        h_ref[at : at + STEP, :] = jnp.maximum(mix(x_ref, at, near1, self1), 0.0).astype(jnp.bfloat16)
    neighbour_sums(h_ref)
    for at in range(0, count * PART, STEP):
        emit(at, mix(h_ref, at, near2, self2).astype(jnp.bfloat16))


def source_kernel(links, packed, near1, self1, near2, self2, out, x_ref, s_ref, h_ref):
    def emit(at, value):
        out[at : at + value.shape[0], :] = value

    graph_layers(
        lambda k: (packed, k),
        lambda k: 7 - k,
        lambda k: links[k],
        near1, self1, near2, self2, x_ref, s_ref, h_ref, emit,
    )


def slot_xor(k):
    b0, b1, b2, b3, b4 = ((k >> bit) & 1 for bit in range(5))
    return ((b0 ^ (3 * b1)) << 3) | ((b2 ^ (3 * b3)) << 1) | b4


SLOT_OF = {slot_xor(k): k for k in range(32)}


def slot_of(v):
    z1, z0, x1, x0, c = ((v >> bit) & 1 for bit in (4, 3, 2, 1, 0))
    return (z0 ^ z1) | (z1 << 1) | ((x0 ^ x1) << 2) | (x1 << 3) | (c << 4)


def spread(row):
    return jnp.transpose(jnp.broadcast_to(row, (LANES, LANES)))


def target_kernel(
    place, own_links, other_links, own, other, near1, self1, near2, self2, emb_source,
    scores, send,
    x_ref, s_ref, h_ref, e_ref,
):
    me = place[0]

    def emit(at, value):
        for piece in range(value.shape[0] // PART):
            q = me ^ slot_xor(at // PART + piece)
            e_ref[pl.ds(pl.multiple_of(q * PART, PART), PART), :] = value[piece * PART : (piece + 1) * PART, :]

    graph_layers(
        lambda k: (own, k) if k < 16 else (other, k - 16),
        lambda k: k ^ SLOT_OF[31],
        lambda k: slot_of((own_links[k] if k < 16 else other_links[k - 16]) ^ me),
        near1, self1, near2, self2, x_ref, s_ref, h_ref, emit,
    )

    for at in range(0, ROWS, 256):
        rows = pl.ds(at, 256)
        top = None
        for i in range(COL_BLOCKS // 2):
            part = lax.dot_general(
                emb_source[rows, :],
                e_ref[i * 256 : (i + 1) * 256, :],
                (((1,), (1,)), ((), ())),
                preferred_element_type=jnp.float32,
            )
            part = 0.2 * part
            scores[2 * i, rows, :] = part[:, :LANES]
            scores[2 * i + 1, rows, :] = part[:, LANES:]
            larger = jnp.maximum(part[:, :LANES], part[:, LANES:])
            top = larger if top is None else jnp.maximum(top, larger)
        total = jnp.exp(scores[0, rows, :] - top)
        for i in range(1, COL_BLOCKS):
            total += jnp.exp(scores[i, rows, :] - top)
        for half in range(2):
            b = at // LANES + half
            part_top = jnp.transpose(top[half * LANES : (half + 1) * LANES])
            part_total = jnp.transpose(total[half * LANES : (half + 1) * LANES])
            larger = jnp.max(part_top, axis=0, keepdims=True)
            part_total = jnp.sum(part_total * jnp.exp(part_top - larger), axis=0, keepdims=True)
            for d in range(N_TGT):
                send[d, b : b + 1, :] = larger
                send[d, b + 4 : b + 5, :] = part_total


def column_kernel(scores, got, weights, tops, lse, potential, shift):
    top, total = got[0, 0:4, :], got[0, 4:8, :]
    larger = top
    for d in range(1, N_TGT):
        larger = jnp.maximum(larger, got[d, 0:4, :])
    total = total * jnp.exp(top - larger)
    for d in range(1, N_TGT):
        total += got[d, 4:8, :] * jnp.exp(got[d, 0:4, :] - larger)
    source = LOG_N - (larger + jnp.log(total))
    potential[0:4, :] = source
    potential[4:8, :] = source
    for b in range(ROW_BLOCKS):
        shift[pl.ds(b * LANES, LANES), :] = spread(source[b : b + 1, :])

    step = 64
    for i in range(COL_BLOCKS):
        top = None
        for at in range(0, ROWS, step):
            rows = pl.ds(at, step)
            x = scores[i, rows, :] + shift[rows, :]
            weights[i, rows, :] = x
            larger = jnp.max(x.reshape(step // 8, 8, LANES), axis=0)
            top = larger if top is None else jnp.maximum(top, larger)
        total = jnp.zeros((8, LANES), jnp.float32)
        for at in range(0, ROWS, step):
            rows = pl.ds(at, step)
            e = jnp.exp(weights[i, rows, :].reshape(step // 8, 8, LANES) - top[None])
            weights[i, rows, :] = e.reshape(step, LANES)
            total += jnp.sum(e, axis=0)
        tops[i] = top
        larger = jnp.max(top, axis=0, keepdims=True)
        total = jnp.sum(total * jnp.exp(top - larger), axis=0, keepdims=True)
        lse[i : i + 1, :] = larger + jnp.log(total)


def row_kernel(weights, tops, got, send, potential, scale):
    larger = got[0]
    for d in range(1, N_PEERS):
        larger = jnp.maximum(larger, got[d])
    total = jnp.exp(got[0] - larger)
    for d in range(1, N_PEERS):
        total += jnp.exp(got[d] - larger)
    target = LOG_N - (larger + jnp.log(total))
    potential[...] = target
    for i in range(COL_BLOCKS):
        scale[i] = jnp.exp(tops[i] + target[i : i + 1, :])
    for b in range(ROW_BLOCKS):
        rows = pl.ds(b * LANES, LANES)
        total = jnp.zeros((LANES // 8, 8, LANES), jnp.float32)
        for i in range(COL_BLOCKS):
            total += weights[i, rows, :].reshape(LANES // 8, 8, LANES) * scale[i][None]
        total = jnp.transpose(total.reshape(LANES, LANES))
        total = jnp.sum(total, axis=0, keepdims=True)
        for d in range(N_TGT):
            send[d, b : b + 1, :] = total
            send[d, b + 4 : b + 5, :] = total


def last_kernel(weights, scale, got, before, sums, potential, factor):
    total = got[0, 0:4, :]
    for d in range(1, N_TGT):
        total += got[d, 0:4, :]
    source = before[0:4, :] + (LOG_N - jnp.log(total))
    potential[0:4, :] = source
    potential[4:8, :] = source
    ratio = 16384.0 / total
    for b in range(ROW_BLOCKS):
        factor[pl.ds(b * LANES, LANES), :] = spread(ratio[b : b + 1, :])

    step = 64
    for i in range(COL_BLOCKS):
        total = jnp.zeros((8, LANES), jnp.float32)
        for at in range(0, ROWS, step):
            rows = pl.ds(at, step)
            e = weights[i, rows, :] * factor[rows, :]
            total += jnp.sum(e.reshape(step // 8, 8, LANES), axis=0)
        sums[i : i + 1, :] = jnp.sum(total * scale[i], axis=0, keepdims=True)


def call(kernel, outs, scratch, ins):
    return pl.pallas_call(
        kernel,
        out_shape=[jax.ShapeDtypeStruct(shape, dtype) for shape, dtype in outs],
        in_specs=ins,
        out_specs=[VMEM() for _ in outs],
        scratch_shapes=scratch,
        compiler_params=pltpu.CompilerParams(vmem_limit_bytes=VMEM_LIMIT),
    )


def swap(value, axis, size, xor):
    return lax.ppermute(value, axis, [(i, i ^ xor) for i in range(size)])


def exchange(value, axes):
    return lax.all_to_all(value, axes, 0, 0)


def on_device(
    source_feats, source_tiles, source_links, target_feats, target_tiles, target_links,
    near_first, self_first, near_second, self_second,
):
    f32, bf16 = jnp.float32, jnp.bfloat16
    weights = (near_first, self_first, near_second, self_second)
    me = lax.axis_index(("zh", "x", "c"))

    held, packed = call(
        pack_kernel,
        [((1, PACK, LANES), bf16), ((N_TGT, PACK, LANES), bf16)],
        [],
        [SMEM()] * 2 + [VMEM()] * 4,
    )(target_links, source_links, target_feats, target_tiles, source_feats, source_tiles)
    for axis, xor in (("zh", 1), ("zh", 3), ("x", 1)):
        held = jnp.concatenate([held, swap(held, axis, 4, xor)], axis=0)
    held, packed = lax.optimization_barrier((held, packed))
    held = jnp.concatenate([held, swap(held, "x", 4, 3)], axis=0)
    packed = exchange(packed, ("y", "zl"))
    held, packed = lax.optimization_barrier((held, packed))
    other = swap(held, "c", 2, 1)
    own_links = held[:, 4 * PART, 0].astype(jnp.int32)
    other_links = swap(own_links, "c", 2, 1)

    source_second = packed[:, 4 * PART, 0].astype(jnp.int32)
    (emb_source,) = call(
        source_kernel,
        [((ROWS, D), bf16)],
        [pltpu.VMEM((ROWS, D), bf16)] * 3,
        [SMEM()] + [VMEM()] * 5,
    )(source_second, packed, *weights)

    scores, send = call(
        target_kernel,
        [((COL_BLOCKS, ROWS, LANES), f32), ((N_TGT, 8, LANES), f32)],
        [pltpu.VMEM((COLS, D), bf16)] * 4,
        [SMEM()] * 3 + [VMEM()] * 7,
    )(me[None], own_links, other_links, held, other, *weights, emb_source)

    got = exchange(send, ("y", "zl"))
    spread_weights, tops, lse, source_first = call(
        column_kernel,
        [
            ((COL_BLOCKS, ROWS, LANES), f32),
            ((COL_BLOCKS, 8, LANES), f32),
            ((COL_BLOCKS, LANES), f32),
            ((8, LANES), f32),
        ],
        [pltpu.VMEM((ROWS, LANES), f32)],
        [VMEM()] * 2,
    )(scores, got)

    lse = jnp.logaddexp(lse, swap(lse, "c", 2, 1))
    got = exchange(jnp.broadcast_to(lse, (N_PEERS, COL_BLOCKS, LANES)), ("zh", "x"))
    send, target_first, scale = call(
        row_kernel,
        [((N_TGT, 8, LANES), f32), ((COL_BLOCKS, LANES), f32), ((COL_BLOCKS, 8, LANES), f32)],
        [],
        [VMEM()] * 3,
    )(spread_weights, tops, got)

    got = exchange(send, ("y", "zl"))
    sums, source_potential = call(
        last_kernel,
        [((COL_BLOCKS, LANES), f32), ((8, LANES), f32)],
        [pltpu.VMEM((ROWS, LANES), f32)],
        [VMEM()] * 4,
    )(spread_weights, scale, got, source_first)

    sums = sums + swap(sums, "c", 2, 1)
    got = exchange(jnp.broadcast_to(sums, (N_PEERS, COL_BLOCKS, LANES)), ("zh", "x"))
    target_potential = target_first + (LOG_N - jnp.log(jnp.sum(got, axis=0)))
    return source_potential[0:4].reshape(ROWS), target_potential.reshape(COLS)


def solution(mesh):
    fine = Mesh(mesh.devices.reshape(4, 4, 2, 4, 2), ("zh", "x", "c", "y", "zl"))
    src, tgt = ("zh", "x", "c"), ("y", "zl")
    return jax.shard_map(
        on_device,
        mesh=fine,
        in_specs=(P(src, tgt, None),) * 3 + (P(tgt, src, None),) * 3 + (P(),) * 4,
        out_specs=(P(src), P(tgt)),
        check_vma=False,
    )
```

```python
import functools
import math

import jax
import jax.numpy as jnp
from jax import lax
from jax.experimental import pallas as pl
from jax.experimental.pallas import tpu as pltpu
from jax.sharding import Mesh, PartitionSpec as P

D = 384
PART = 64
PACK = 272
ROWS = 512
COLS = 2048
LANES = 128
ROW_BLOCKS = ROWS // LANES
COL_BLOCKS = COLS // LANES
N_TGT = 8
STEP = 512
N_PEERS = 16
LOG_N = math.log(16384.0)
VMEM_LIMIT = 32 * 1024 * 1024
PACK_LIMIT = 60 * 1024 * 1024

VMEM = functools.partial(pl.BlockSpec, memory_space=pltpu.VMEM)
HBM = functools.partial(pl.BlockSpec, memory_space=pltpu.HBM)
SMEM = functools.partial(pl.BlockSpec, memory_space=pltpu.SMEM)


def pack_kernel(feats, tiles, links, out, feats_ref, tiles_ref, links_ref, sems):
    pairs = ((feats, feats_ref), (tiles, tiles_ref), (links, links_ref))
    copies = [pltpu.make_async_copy(src, dst, sems.at[i]) for i, (src, dst) in enumerate(pairs)]
    for copy in copies:
        copy.start()
    for copy in copies:
        copy.wait()
    link = jnp.broadcast_to(links_ref[0, 0:1, 1:2].astype(jnp.float32), (16, LANES)).astype(jnp.bfloat16)
    for d in range(out.shape[0]):
        for piece in range(D // LANES):
            out[d, piece * PART : (piece + 1) * PART, :] = feats_ref[0, :, piece * LANES : (piece + 1) * LANES]
        out[d, 3 * PART : 4 * PART, :] = tiles_ref[0]
        out[d, 4 * PART : PACK, :] = link


def pack(feats, tiles, links, count):
    (packed,) = call(
        pack_kernel,
        [((count, PACK, LANES), jnp.bfloat16)],
        [pltpu.VMEM(v.shape, v.dtype) for v in (feats, tiles, links)] + [pltpu.SemaphoreType.DMA((3,))],
        [HBM()] * 3,
        limit=PACK_LIMIT,
    )(feats, tiles, links)
    return packed


def graph_layers(packed, first, second, near1, self1, near2, self2, x_ref, s_ref, h_ref, emit):
    count = x_ref.shape[0] // PART
    for k in range(count):
        ref, at = packed(k)
        for piece in range(D // LANES):
            x_ref[k * PART : (k + 1) * PART, piece * LANES : (piece + 1) * LANES] = ref[
                at, piece * PART : (piece + 1) * PART, :
            ]

    def neighbour_sums(src):
        for k in range(count):
            ref, at = packed(k)
            near = src[pl.ds(first(k) * PART, PART), :]
            other = src[pl.ds(pl.multiple_of(second(k) * PART, PART), PART), :]
            panel = ref[at, 3 * PART : 4 * PART, :]
            both = jnp.concatenate([near, other], axis=0)
            total = jnp.dot(panel, both, preferred_element_type=jnp.float32)
            s_ref[k * PART : (k + 1) * PART, :] = total.astype(jnp.bfloat16)

    def mix(src, at, near, own):
        left = jnp.concatenate([s_ref[at : at + STEP, :], src[at : at + STEP, :]], axis=1)
        right = jnp.concatenate([near[...], own[...]], axis=0)
        return jnp.dot(left, right, preferred_element_type=jnp.float32)

    neighbour_sums(x_ref)
    for at in range(0, count * PART, STEP):
        h_ref[at : at + STEP, :] = jnp.maximum(mix(x_ref, at, near1, self1), 0.0).astype(jnp.bfloat16)
    neighbour_sums(h_ref)
    for at in range(0, count * PART, STEP):
        emit(at, mix(h_ref, at, near2, self2).astype(jnp.bfloat16))


def source_kernel(links, packed, near1, self1, near2, self2, out, x_ref, s_ref, h_ref):
    def emit(at, value):
        out[at : at + value.shape[0], :] = value

    graph_layers(
        lambda k: (packed, k),
        lambda k: 7 - k,
        lambda k: links[k],
        near1, self1, near2, self2, x_ref, s_ref, h_ref, emit,
    )


def slot_xor(k):
    return ((k & 3) << 3) | (((k >> 2) & 3) << 1) | (k >> 4)


def slot_of(v):
    return (v >> 3) | (((v >> 1) & 3) << 2) | ((v & 1) << 4)


def spread(row):
    return jnp.transpose(jnp.broadcast_to(row, (LANES, LANES)))


def target_kernel(
    place, own_links, other_links,
    own0, own1, own2, own3, other0, other1, other2, other3,
    near1, self1, near2, self2, emb_source,
    scores, send,
    x_ref, s_ref, h_ref, e_ref,
):
    me = place[0]
    pieces = (own0, own1, own2, own3, other0, other1, other2, other3)

    def emit(at, value):
        for piece in range(value.shape[0] // PART):
            q = me ^ slot_xor(at // PART + piece)
            e_ref[pl.ds(pl.multiple_of(q * PART, PART), PART), :] = value[piece * PART : (piece + 1) * PART, :]

    graph_layers(
        lambda k: (pieces[k // 4], k % 4),
        lambda k: k ^ 31,
        lambda k: slot_of((own_links[k] if k < 16 else other_links[k - 16]) ^ me),
        near1, self1, near2, self2, x_ref, s_ref, h_ref, emit,
    )

    for at in range(0, ROWS, 256):
        rows = pl.ds(at, 256)
        top = None
        for i in range(COL_BLOCKS // 2):
            part = lax.dot_general(
                emb_source[rows, :],
                e_ref[i * 256 : (i + 1) * 256, :],
                (((1,), (1,)), ((), ())),
                preferred_element_type=jnp.float32,
            )
            part = 0.2 * part
            scores[2 * i, rows, :] = part[:, :LANES]
            scores[2 * i + 1, rows, :] = part[:, LANES:]
            larger = jnp.maximum(part[:, :LANES], part[:, LANES:])
            top = larger if top is None else jnp.maximum(top, larger)
        total = jnp.exp(scores[0, rows, :] - top)
        for i in range(1, COL_BLOCKS):
            total += jnp.exp(scores[i, rows, :] - top)
        for half in range(2):
            b = at // LANES + half
            part_top = jnp.transpose(top[half * LANES : (half + 1) * LANES])
            part_total = jnp.transpose(total[half * LANES : (half + 1) * LANES])
            larger = jnp.max(part_top, axis=0, keepdims=True)
            part_total = jnp.sum(part_total * jnp.exp(part_top - larger), axis=0, keepdims=True)
            for d in range(N_TGT):
                send[d, b : b + 1, :] = larger
                send[d, b + 4 : b + 5, :] = part_total


def column_kernel(scores, got, weights, tops, lse, potential, shift):
    top, total = got[0, 0:4, :], got[0, 4:8, :]
    larger = top
    for d in range(1, N_TGT):
        larger = jnp.maximum(larger, got[d, 0:4, :])
    total = total * jnp.exp(top - larger)
    for d in range(1, N_TGT):
        total += got[d, 4:8, :] * jnp.exp(got[d, 0:4, :] - larger)
    source = LOG_N - (larger + jnp.log(total))
    potential[0:4, :] = source
    potential[4:8, :] = source
    for b in range(ROW_BLOCKS):
        shift[pl.ds(b * LANES, LANES), :] = spread(source[b : b + 1, :])

    step = 64
    for i in range(COL_BLOCKS):
        top = None
        for at in range(0, ROWS, step):
            rows = pl.ds(at, step)
            x = scores[i, rows, :] + shift[rows, :]
            weights[i, rows, :] = x
            larger = jnp.max(x.reshape(step // 8, 8, LANES), axis=0)
            top = larger if top is None else jnp.maximum(top, larger)
        total = jnp.zeros((8, LANES), jnp.float32)
        for at in range(0, ROWS, step):
            rows = pl.ds(at, step)
            e = jnp.exp(weights[i, rows, :].reshape(step // 8, 8, LANES) - top[None])
            weights[i, rows, :] = e.reshape(step, LANES)
            total += jnp.sum(e, axis=0)
        tops[i] = top
        larger = jnp.max(top, axis=0, keepdims=True)
        total = jnp.sum(total * jnp.exp(top - larger), axis=0, keepdims=True)
        lse[i : i + 1, :] = larger + jnp.log(total)


def row_kernel(weights, tops, got, send, potential, scale):
    larger = got[0]
    for d in range(1, N_PEERS):
        larger = jnp.maximum(larger, got[d])
    total = jnp.exp(got[0] - larger)
    for d in range(1, N_PEERS):
        total += jnp.exp(got[d] - larger)
    target = LOG_N - (larger + jnp.log(total))
    potential[...] = target
    for i in range(COL_BLOCKS):
        scale[i] = jnp.exp(tops[i] + target[i : i + 1, :])
    for b in range(ROW_BLOCKS):
        rows = pl.ds(b * LANES, LANES)
        total = jnp.zeros((LANES // 8, 8, LANES), jnp.float32)
        for i in range(COL_BLOCKS):
            total += weights[i, rows, :].reshape(LANES // 8, 8, LANES) * scale[i][None]
        total = jnp.transpose(total.reshape(LANES, LANES))
        total = jnp.sum(total, axis=0, keepdims=True)
        for d in range(N_TGT):
            send[d, b : b + 1, :] = total
            send[d, b + 4 : b + 5, :] = total


def last_kernel(weights, scale, got, before, sums, potential, factor):
    total = got[0, 0:4, :]
    for d in range(1, N_TGT):
        total += got[d, 0:4, :]
    source = before[0:4, :] + (LOG_N - jnp.log(total))
    potential[0:4, :] = source
    potential[4:8, :] = source
    ratio = 16384.0 / total
    for b in range(ROW_BLOCKS):
        factor[pl.ds(b * LANES, LANES), :] = spread(ratio[b : b + 1, :])

    step = 64
    for i in range(COL_BLOCKS):
        total = jnp.zeros((8, LANES), jnp.float32)
        for at in range(0, ROWS, step):
            rows = pl.ds(at, step)
            e = weights[i, rows, :] * factor[rows, :]
            total += jnp.sum(e.reshape(step // 8, 8, LANES), axis=0)
        sums[i : i + 1, :] = jnp.sum(total * scale[i], axis=0, keepdims=True)


def call(kernel, outs, scratch, ins, cost=None, limit=VMEM_LIMIT):
    return pl.pallas_call(
        kernel,
        out_shape=[jax.ShapeDtypeStruct(shape, dtype) for shape, dtype in outs],
        in_specs=ins,
        out_specs=[VMEM() for _ in outs],
        scratch_shapes=scratch,
        cost_estimate=cost,
        compiler_params=pltpu.CompilerParams(vmem_limit_bytes=limit),
    )


def swap(value, axis, size, xor):
    return lax.ppermute(value, axis, [(i, i ^ xor) for i in range(size)])


def exchange(value, axes):
    return lax.all_to_all(value, axes, 0, 0)


def on_device(
    source_feats, source_tiles, source_links, target_feats, target_tiles, target_links,
    near_first, self_first, near_second, self_second,
):
    f32, bf16 = jnp.float32, jnp.bfloat16
    weights = (near_first, self_first, near_second, self_second)
    me = lax.axis_index(("zh", "x", "c"))

    held = pack(target_feats, target_tiles, target_links, 1)
    packed = pack(source_feats, source_tiles, source_links, N_TGT)
    near, far, beyond = (swap(held, "zh", 4, xor) for xor in (1, 2, 3))
    near, packed = lax.optimization_barrier((near, packed))
    packed = exchange(packed, ("y", "zl"))
    held = jnp.concatenate([held, near, far, beyond], axis=0)
    own = [held] + [swap(held, "x", 4, xor) for xor in (1, 2, 3)]
    other = [swap(piece, "c", 2, 1) for piece in own]
    own_links = jnp.concatenate([piece[:, 4 * PART, 0] for piece in own]).astype(jnp.int32)
    other_links = swap(own_links, "c", 2, 1)

    source_second = packed[:, 4 * PART, 0].astype(jnp.int32)
    (emb_source,) = call(
        source_kernel,
        [((ROWS, D), bf16)],
        [pltpu.VMEM((ROWS, D), bf16)] * 3,
        [SMEM()] + [VMEM()] * 5,
        pl.CostEstimate(flops=700_000_000, bytes_accessed=2_000_000, transcendentals=0),
    )(source_second, packed, *weights)

    scores, send = call(
        target_kernel,
        [((COL_BLOCKS, ROWS, LANES), f32), ((N_TGT, 8, LANES), f32)],
        [pltpu.VMEM((COLS, D), bf16)] * 4,
        [SMEM()] * 3 + [VMEM()] * 13,
    )(me[None], own_links, other_links, *own, *other, *weights, emb_source)

    got = exchange(send, ("y", "zl"))
    spread_weights, tops, lse, source_first = call(
        column_kernel,
        [
            ((COL_BLOCKS, ROWS, LANES), f32),
            ((COL_BLOCKS, 8, LANES), f32),
            ((COL_BLOCKS, LANES), f32),
            ((8, LANES), f32),
        ],
        [pltpu.VMEM((ROWS, LANES), f32)],
        [VMEM()] * 2,
    )(scores, got)

    lse = jnp.logaddexp(lse, swap(lse, "c", 2, 1))
    got = exchange(jnp.broadcast_to(lse, (N_PEERS, COL_BLOCKS, LANES)), ("zh", "x"))
    send, target_first, scale = call(
        row_kernel,
        [((N_TGT, 8, LANES), f32), ((COL_BLOCKS, LANES), f32), ((COL_BLOCKS, 8, LANES), f32)],
        [],
        [VMEM()] * 3,
    )(spread_weights, tops, got)

    got = exchange(send, ("y", "zl"))
    sums, source_potential = call(
        last_kernel,
        [((COL_BLOCKS, LANES), f32), ((8, LANES), f32)],
        [pltpu.VMEM((ROWS, LANES), f32)],
        [VMEM()] * 4,
    )(spread_weights, scale, got, source_first)

    sums = sums + swap(sums, "c", 2, 1)
    got = exchange(jnp.broadcast_to(sums, (N_PEERS, COL_BLOCKS, LANES)), ("zh", "x"))
    target_potential = target_first + (LOG_N - jnp.log(jnp.sum(got, axis=0)))
    return source_potential[0:4].reshape(ROWS), target_potential.reshape(COLS)


def solution(mesh):
    fine = Mesh(mesh.devices.reshape(4, 4, 2, 4, 2), ("zh", "x", "c", "y", "zl"))
    src, tgt = ("zh", "x", "c"), ("y", "zl")
    return jax.shard_map(
        on_device,
        mesh=fine,
        in_specs=(P(src, tgt, None),) * 3 + (P(tgt, src, None),) * 3 + (P(),) * 4,
        out_specs=(P(src), P(tgt)),
        check_vma=False,
    )
```

```python
import functools
import math

import jax
import jax.numpy as jnp
from jax import lax
from jax.experimental import pallas as pl
from jax.experimental.pallas import tpu as pltpu
from jax.sharding import Mesh, PartitionSpec as P

D = 384
PART = 64
PACK = 272
ROWS = 512
COLS = 2048
LANES = 128
ROW_BLOCKS = ROWS // LANES
COL_BLOCKS = COLS // LANES
N_TGT = 8
STEP = 512
N_PEERS = 16
LOG_N = math.log(16384.0)
VMEM_LIMIT = 32 * 1024 * 1024
PACK_LIMIT = 60 * 1024 * 1024

VMEM = functools.partial(pl.BlockSpec, memory_space=pltpu.VMEM)
HBM = functools.partial(pl.BlockSpec, memory_space=pltpu.HBM)
SMEM = functools.partial(pl.BlockSpec, memory_space=pltpu.SMEM)


def pack_kernel(feats, tiles, links, out, feats_ref, tiles_ref, links_ref, sems):
    pairs = ((feats, feats_ref), (tiles, tiles_ref), (links, links_ref))
    copies = [pltpu.make_async_copy(src, dst, sems.at[i]) for i, (src, dst) in enumerate(pairs)]
    for copy in copies:
        copy.start()
    for copy in copies:
        copy.wait()
    for piece in range(D // LANES):
        out[0, piece * PART : (piece + 1) * PART, :] = feats_ref[0, :, piece * LANES : (piece + 1) * LANES]
    out[0, 3 * PART : 4 * PART, :] = tiles_ref[0]
    link = jnp.broadcast_to(links_ref[0, 0:1, 1:2].astype(jnp.float32), (16, LANES))
    out[0, 4 * PART : PACK, :] = link.astype(jnp.bfloat16)


def pack(feats, tiles, links):
    (packed,) = call(
        pack_kernel,
        [((1, PACK, LANES), jnp.bfloat16)],
        [pltpu.VMEM(v.shape, v.dtype) for v in (feats, tiles, links)] + [pltpu.SemaphoreType.DMA((3,))],
        [HBM()] * 3,
        limit=PACK_LIMIT,
    )(feats, tiles, links)
    return packed


def graph_layers(packed, first, second, weights, x_ref, s_ref, h_ref, emit):
    count = x_ref.shape[0] // PART
    for k in range(count):
        ref, at = packed(k)
        for piece in range(D // LANES):
            x_ref[k * PART : (k + 1) * PART, piece * LANES : (piece + 1) * LANES] = ref[
                at, piece * PART : (piece + 1) * PART, :
            ]

    def neighbour_sums(src):
        for k in range(count):
            ref, at = packed(k)
            near = src[pl.ds(first(k) * PART, PART), :]
            other = src[pl.ds(pl.multiple_of(second(k) * PART, PART), PART), :]
            panel = ref[at, 3 * PART : 4 * PART, :]
            both = jnp.concatenate([near, other], axis=0)
            total = jnp.dot(panel, both, preferred_element_type=jnp.float32)
            s_ref[k * PART : (k + 1) * PART, :] = total.astype(jnp.bfloat16)

    def mix(src, at, layer):
        left = jnp.concatenate([s_ref[at : at + STEP, :], src[at : at + STEP, :]], axis=1)
        right = weights[layer * 2 * D : (layer + 1) * 2 * D, :]
        return jnp.dot(left, right, preferred_element_type=jnp.float32)

    neighbour_sums(x_ref)
    for at in range(0, count * PART, STEP):
        h_ref[at : at + STEP, :] = jnp.maximum(mix(x_ref, at, 0), 0.0).astype(jnp.bfloat16)
    neighbour_sums(h_ref)
    for at in range(0, count * PART, STEP):
        emit(at, mix(h_ref, at, 1).astype(jnp.bfloat16))


def source_kernel(place, links, own0, own1, own2, own3, weights, out, x_ref, s_ref, h_ref):
    me = place[0]
    pieces = (own0, own1, own2, own3)

    def emit(at, value):
        for k in range(value.shape[0] // PART):
            q = me ^ (at // PART + k)
            out[pl.ds(pl.multiple_of(q * PART, PART), PART), :] = value[k * PART : (k + 1) * PART, :]

    graph_layers(
        lambda k: (pieces[k // 2], k % 2),
        lambda k: k ^ 7,
        lambda k: links[k] ^ me,
        weights, x_ref, s_ref, h_ref, emit,
    )


def slot_xor(k):
    return ((k & 3) << 3) | (((k >> 2) & 3) << 1) | (k >> 4)


def slot_of(v):
    return (v >> 3) | (((v >> 1) & 3) << 2) | ((v & 1) << 4)


def spread(row):
    return jnp.transpose(jnp.broadcast_to(row, (LANES, LANES)))


def target_kernel(
    place, own_links, other_links,
    own0, own1, own2, own3, other0, other1, other2, other3,
    weights, emb_source,
    scores, send,
    x_ref, s_ref, h_ref, e_ref,
):
    me = place[0]
    pieces = (own0, own1, own2, own3, other0, other1, other2, other3)

    def emit(at, value):
        for piece in range(value.shape[0] // PART):
            q = me ^ slot_xor(at // PART + piece)
            e_ref[pl.ds(pl.multiple_of(q * PART, PART), PART), :] = value[piece * PART : (piece + 1) * PART, :]

    graph_layers(
        lambda k: (pieces[k // 4], k % 4),
        lambda k: k ^ 31,
        lambda k: slot_of((own_links[k] if k < 16 else other_links[k - 16]) ^ me),
        weights, x_ref, s_ref, h_ref, emit,
    )

    for at in range(0, ROWS, 256):
        rows = pl.ds(at, 256)
        top = None
        for i in range(COL_BLOCKS // 2):
            part = lax.dot_general(
                emb_source[rows, :],
                e_ref[i * 256 : (i + 1) * 256, :],
                (((1,), (1,)), ((), ())),
                preferred_element_type=jnp.float32,
            )
            part = 0.2 * part
            scores[2 * i, rows, :] = part[:, :LANES]
            scores[2 * i + 1, rows, :] = part[:, LANES:]
            larger = jnp.maximum(part[:, :LANES], part[:, LANES:])
            top = larger if top is None else jnp.maximum(top, larger)
        total = jnp.exp(scores[0, rows, :] - top)
        for i in range(1, COL_BLOCKS):
            total += jnp.exp(scores[i, rows, :] - top)
        for half in range(2):
            b = at // LANES + half
            part_top = jnp.transpose(top[half * LANES : (half + 1) * LANES])
            part_total = jnp.transpose(total[half * LANES : (half + 1) * LANES])
            larger = jnp.max(part_top, axis=0, keepdims=True)
            part_total = jnp.sum(part_total * jnp.exp(part_top - larger), axis=0, keepdims=True)
            for d in range(N_TGT):
                send[d, b : b + 1, :] = larger
                send[d, b + 4 : b + 5, :] = part_total


def column_kernel(scores, got, weights, tops, lse, potential, shift):
    top, total = got[0, 0:4, :], got[0, 4:8, :]
    larger = top
    for d in range(1, N_TGT):
        larger = jnp.maximum(larger, got[d, 0:4, :])
    total = total * jnp.exp(top - larger)
    for d in range(1, N_TGT):
        total += got[d, 4:8, :] * jnp.exp(got[d, 0:4, :] - larger)
    source = LOG_N - (larger + jnp.log(total))
    potential[0:4, :] = source
    potential[4:8, :] = source
    for b in range(ROW_BLOCKS):
        shift[pl.ds(b * LANES, LANES), :] = spread(source[b : b + 1, :])

    step = 64
    for i in range(COL_BLOCKS):
        top = None
        for at in range(0, ROWS, step):
            rows = pl.ds(at, step)
            x = scores[i, rows, :] + shift[rows, :]
            weights[i, rows, :] = x
            larger = jnp.max(x.reshape(step // 8, 8, LANES), axis=0)
            top = larger if top is None else jnp.maximum(top, larger)
        total = jnp.zeros((8, LANES), jnp.float32)
        for at in range(0, ROWS, step):
            rows = pl.ds(at, step)
            e = jnp.exp(weights[i, rows, :].reshape(step // 8, 8, LANES) - top[None])
            weights[i, rows, :] = e.reshape(step, LANES)
            total += jnp.sum(e, axis=0)
        tops[i] = top
        larger = jnp.max(top, axis=0, keepdims=True)
        total = jnp.sum(total * jnp.exp(top - larger), axis=0, keepdims=True)
        lse[i : i + 1, :] = larger + jnp.log(total)


def row_kernel(weights, tops, got, send, potential, scale):
    larger = got[0]
    for d in range(1, N_PEERS):
        larger = jnp.maximum(larger, got[d])
    total = jnp.exp(got[0] - larger)
    for d in range(1, N_PEERS):
        total += jnp.exp(got[d] - larger)
    target = LOG_N - (larger + jnp.log(total))
    potential[...] = target
    for i in range(COL_BLOCKS):
        scale[i] = jnp.exp(tops[i] + target[i : i + 1, :])
    for b in range(ROW_BLOCKS):
        rows = pl.ds(b * LANES, LANES)
        total = jnp.zeros((LANES // 8, 8, LANES), jnp.float32)
        for i in range(COL_BLOCKS):
            total += weights[i, rows, :].reshape(LANES // 8, 8, LANES) * scale[i][None]
        total = jnp.transpose(total.reshape(LANES, LANES))
        total = jnp.sum(total, axis=0, keepdims=True)
        for d in range(N_TGT):
            send[d, b : b + 1, :] = total
            send[d, b + 4 : b + 5, :] = total


def last_kernel(weights, scale, got, before, sums, potential, factor):
    total = got[0, 0:4, :]
    for d in range(1, N_TGT):
        total += got[d, 0:4, :]
    source = before[0:4, :] + (LOG_N - jnp.log(total))
    potential[0:4, :] = source
    potential[4:8, :] = source
    ratio = 16384.0 / total
    for b in range(ROW_BLOCKS):
        factor[pl.ds(b * LANES, LANES), :] = spread(ratio[b : b + 1, :])

    step = 64
    for i in range(COL_BLOCKS):
        total = jnp.zeros((8, LANES), jnp.float32)
        for at in range(0, ROWS, step):
            rows = pl.ds(at, step)
            e = weights[i, rows, :] * factor[rows, :]
            total += jnp.sum(e.reshape(step // 8, 8, LANES), axis=0)
        total = jnp.sum(total * scale[i], axis=0, keepdims=True)
        for d in range(N_PEERS):
            sums[d, i : i + 1, :] = total


def call(kernel, outs, scratch, ins, cost=None, limit=VMEM_LIMIT):
    return pl.pallas_call(
        kernel,
        out_shape=[jax.ShapeDtypeStruct(shape, dtype) for shape, dtype in outs],
        in_specs=ins,
        out_specs=[VMEM() for _ in outs],
        scratch_shapes=scratch,
        cost_estimate=cost,
        compiler_params=pltpu.CompilerParams(vmem_limit_bytes=limit),
    )


def swap(value, axis, size, xor):
    return lax.ppermute(value, axis, [(i, i ^ xor) for i in range(size)])


def exchange(value, axes):
    return lax.all_to_all(value, axes, 0, 0)


def on_device(
    source_feats, source_tiles, source_links, target_feats, target_tiles, target_links,
    near_first, self_first, near_second, self_second,
):
    f32, bf16 = jnp.float32, jnp.bfloat16
    me = lax.axis_index(("zh", "x", "c"))
    me_source = lax.axis_index(("y", "zl"))

    held = pack(target_feats, target_tiles, target_links)
    source = pack(source_feats, source_tiles, source_links)
    held, source, *weights = lax.optimization_barrier(
        (held, source, near_first, self_first, near_second, self_second)
    )
    weights = jnp.concatenate(weights, axis=0)
    held = jnp.concatenate([held] + [swap(held, "zh", 4, xor) for xor in (1, 2, 3)], axis=0)
    source = jnp.concatenate([source, swap(source, "zl", 2, 1)], axis=0)
    held, source, weights = lax.optimization_barrier((held, source, weights))
    own = [held] + [swap(held, "x", 4, xor) for xor in (1, 2, 3)]
    source = [source] + [swap(source, "y", 4, xor) for xor in (1, 2, 3)]
    other = [swap(piece, "c", 2, 1) for piece in own]
    own_links = jnp.concatenate([piece[:, 4 * PART, 0] for piece in own]).astype(jnp.int32)
    other_links = swap(own_links, "c", 2, 1)

    (emb_source,) = call(
        source_kernel,
        [((ROWS, D), bf16)],
        [pltpu.VMEM((ROWS, D), bf16)] * 3,
        [SMEM()] * 2 + [VMEM()] * 5,
        pl.CostEstimate(flops=700_000_000, bytes_accessed=2_000_000, transcendentals=0),
    )(
        me_source[None],
        jnp.concatenate([piece[:, 4 * PART, 0] for piece in source]).astype(jnp.int32),
        *source,
        weights,
    )

    scores, send = call(
        target_kernel,
        [((COL_BLOCKS, ROWS, LANES), f32), ((N_TGT, 8, LANES), f32)],
        [pltpu.VMEM((COLS, D), bf16)] * 4,
        [SMEM()] * 3 + [VMEM()] * 10,
    )(me[None], own_links, other_links, *own, *other, weights, emb_source)

    got = exchange(send, ("y", "zl"))
    spread_weights, tops, lse, source_first = call(
        column_kernel,
        [
            ((COL_BLOCKS, ROWS, LANES), f32),
            ((COL_BLOCKS, 8, LANES), f32),
            ((COL_BLOCKS, LANES), f32),
            ((8, LANES), f32),
        ],
        [pltpu.VMEM((ROWS, LANES), f32)],
        [VMEM()] * 2,
    )(scores, got)

    lse = jnp.logaddexp(lse, swap(lse, "c", 2, 1))
    got = exchange(jnp.broadcast_to(lse, (N_PEERS, COL_BLOCKS, LANES)), ("zh", "x"))
    send, target_first, scale = call(
        row_kernel,
        [((N_TGT, 8, LANES), f32), ((COL_BLOCKS, LANES), f32), ((COL_BLOCKS, 8, LANES), f32)],
        [],
        [VMEM()] * 3,
    )(spread_weights, tops, got)

    got = exchange(send, ("y", "zl"))
    sums, source_potential = call(
        last_kernel,
        [((N_PEERS, COL_BLOCKS, LANES), f32), ((8, LANES), f32)],
        [pltpu.VMEM((ROWS, LANES), f32)],
        [VMEM()] * 4,
    )(spread_weights, scale, got, source_first)

    total = jnp.sum(exchange(sums, ("zh", "x")), axis=0)
    total = total + swap(total, "c", 2, 1)
    target_potential = target_first + (LOG_N - jnp.log(total))
    return source_potential[0:4].reshape(ROWS), target_potential.reshape(COLS)


def solution(mesh):
    fine = Mesh(mesh.devices.reshape(4, 4, 2, 4, 2), ("zh", "x", "c", "y", "zl"))
    src, tgt = ("zh", "x", "c"), ("y", "zl")
    return jax.shard_map(
        on_device,
        mesh=fine,
        in_specs=(P(src, tgt, None),) * 3 + (P(tgt, src, None),) * 3 + (P(),) * 4,
        out_specs=(P(src), P(tgt)),
        check_vma=False,
    )
```

```python
import functools
import math

import jax
import jax.numpy as jnp
from jax import lax
from jax.experimental import pallas as pl
from jax.experimental.pallas import tpu as pltpu
from jax.sharding import Mesh, PartitionSpec as P

D = 384
PART = 64
PACK = 272
ROWS = 512
COLS = 2048
LANES = 128
ROW_BLOCKS = ROWS // LANES
COL_BLOCKS = COLS // LANES
N_TGT = 8
STEP = 512
N_PEERS = 16
LOG_N = math.log(16384.0)
VMEM_LIMIT = 32 * 1024 * 1024
PACK_LIMIT = 60 * 1024 * 1024

VMEM = functools.partial(pl.BlockSpec, memory_space=pltpu.VMEM)
HBM = functools.partial(pl.BlockSpec, memory_space=pltpu.HBM)
SMEM = functools.partial(pl.BlockSpec, memory_space=pltpu.SMEM)


def pack_kernel(*refs):
    sources, outs, held, sems = refs[:6], refs[6:8], refs[8:14], refs[14]
    copies = [pltpu.make_async_copy(src, dst, sems.at[i]) for i, (src, dst) in enumerate(zip(sources, held))]
    for copy in copies:
        copy.start()
    for graph, out in enumerate(outs):
        for copy in copies[3 * graph : 3 * graph + 3]:
            copy.wait()
        feats, tiles, links = held[3 * graph : 3 * graph + 3]
        for piece in range(D // LANES):
            out[0, piece * PART : (piece + 1) * PART, :] = feats[0, :, piece * LANES : (piece + 1) * LANES]
        out[0, 3 * PART : 4 * PART, :] = tiles[0]
        link = jnp.broadcast_to(links[0, 0:1, 1:2].astype(jnp.float32), (16, LANES))
        out[0, 4 * PART : PACK, :] = link.astype(jnp.bfloat16)


def pack(*arrays):
    return call(
        pack_kernel,
        [((1, PACK, LANES), jnp.bfloat16)] * 2,
        [pltpu.VMEM(v.shape, v.dtype) for v in arrays] + [pltpu.SemaphoreType.DMA((6,))],
        [HBM()] * 6,
        limit=PACK_LIMIT,
    )(*arrays)


def graph_layers(packed, first, second, weights, x_ref, s_ref, h_ref, emit):
    count = x_ref.shape[0] // PART
    for k in range(count):
        ref, at = packed(k)
        for piece in range(D // LANES):
            x_ref[k * PART : (k + 1) * PART, piece * LANES : (piece + 1) * LANES] = ref[
                at, piece * PART : (piece + 1) * PART, :
            ]

    def neighbour_sums(src):
        for k in range(count):
            ref, at = packed(k)
            near = src[pl.ds(first(k) * PART, PART), :]
            other = src[pl.ds(pl.multiple_of(second(k) * PART, PART), PART), :]
            panel = ref[at, 3 * PART : 4 * PART, :]
            both = jnp.concatenate([near, other], axis=0)
            total = jnp.dot(panel, both, preferred_element_type=jnp.float32)
            s_ref[k * PART : (k + 1) * PART, :] = total.astype(jnp.bfloat16)

    def mix(src, at, layer):
        left = jnp.concatenate([s_ref[at : at + STEP, :], src[at : at + STEP, :]], axis=1)
        right = weights[layer * 2 * D : (layer + 1) * 2 * D, :]
        return jnp.dot(left, right, preferred_element_type=jnp.float32)

    neighbour_sums(x_ref)
    for at in range(0, count * PART, STEP):
        h_ref[at : at + STEP, :] = jnp.maximum(mix(x_ref, at, 0), 0.0).astype(jnp.bfloat16)
    neighbour_sums(h_ref)
    for at in range(0, count * PART, STEP):
        emit(at, mix(h_ref, at, 1).astype(jnp.bfloat16))


def turn(v):
    return ((v & 1) << 1) | (v >> 1)


def slot_xor(k):
    return (turn(k & 3) << 3) | (turn((k >> 2) & 3) << 1) | (k >> 4)


def slot_of(v):
    return turn(v >> 3) | (turn((v >> 1) & 3) << 2) | ((v & 1) << 4)


def source_kernel(place, links, own0, own1, own2, own3, weights, out, x_ref, s_ref, h_ref):
    me = place[0]
    pieces = (own0, own1, own2, own3)

    def emit(at, value):
        for k in range(value.shape[0] // PART):
            slot = at // PART + k
            q = me ^ ((turn(slot >> 1) << 1) | (slot & 1))
            out[pl.ds(pl.multiple_of(q * PART, PART), PART), :] = value[k * PART : (k + 1) * PART, :]

    graph_layers(
        lambda k: (pieces[k // 2], k % 2),
        lambda k: k ^ 7,
        lambda k: (turn((links[k] ^ me) >> 1) << 1) | ((links[k] ^ me) & 1),
        weights, x_ref, s_ref, h_ref, emit,
    )


def spread(row):
    return jnp.transpose(jnp.broadcast_to(row, (LANES, LANES)))


def target_kernel(
    place, own_links, other_links,
    own0, own1, own2, own3, other0, other1, other2, other3,
    weights, emb_source,
    scores, send,
    x_ref, s_ref, h_ref, e_ref,
):
    me = place[0]
    pieces = (own0, own1, own2, own3, other0, other1, other2, other3)

    def emit(at, value):
        for piece in range(value.shape[0] // PART):
            q = me ^ slot_xor(at // PART + piece)
            e_ref[pl.ds(pl.multiple_of(q * PART, PART), PART), :] = value[piece * PART : (piece + 1) * PART, :]

    graph_layers(
        lambda k: (pieces[k // 4], k % 4),
        lambda k: k ^ 31,
        lambda k: slot_of((own_links[k] if k < 16 else other_links[k - 16]) ^ me),
        weights, x_ref, s_ref, h_ref, emit,
    )

    for at in range(0, ROWS, 256):
        rows = pl.ds(at, 256)
        top = None
        for i in range(COL_BLOCKS // 2):
            part = lax.dot_general(
                emb_source[rows, :],
                e_ref[i * 256 : (i + 1) * 256, :],
                (((1,), (1,)), ((), ())),
                preferred_element_type=jnp.float32,
            )
            part = 0.2 * part
            scores[2 * i, rows, :] = part[:, :LANES]
            scores[2 * i + 1, rows, :] = part[:, LANES:]
            larger = jnp.maximum(part[:, :LANES], part[:, LANES:])
            top = larger if top is None else jnp.maximum(top, larger)
        total = jnp.exp(scores[0, rows, :] - top)
        for i in range(1, COL_BLOCKS):
            total += jnp.exp(scores[i, rows, :] - top)
        for half in range(2):
            b = at // LANES + half
            part_top = jnp.transpose(top[half * LANES : (half + 1) * LANES])
            part_total = jnp.transpose(total[half * LANES : (half + 1) * LANES])
            larger = jnp.max(part_top, axis=0, keepdims=True)
            part_total = jnp.sum(part_total * jnp.exp(part_top - larger), axis=0, keepdims=True)
            for d in range(N_TGT):
                send[d, b : b + 1, :] = larger
                send[d, b + 4 : b + 5, :] = part_total


def column_kernel(scores, got, weights, tops, lse, potential, shift):
    top, total = got[0, 0:4, :], got[0, 4:8, :]
    larger = top
    for d in range(1, N_TGT):
        larger = jnp.maximum(larger, got[d, 0:4, :])
    total = total * jnp.exp(top - larger)
    for d in range(1, N_TGT):
        total += got[d, 4:8, :] * jnp.exp(got[d, 0:4, :] - larger)
    source = LOG_N - (larger + jnp.log(total))
    potential[0:4, :] = source
    potential[4:8, :] = source
    for b in range(ROW_BLOCKS):
        shift[pl.ds(b * LANES, LANES), :] = spread(source[b : b + 1, :])

    step = 64
    for i in range(COL_BLOCKS):
        top = None
        for at in range(0, ROWS, step):
            rows = pl.ds(at, step)
            x = scores[i, rows, :] + shift[rows, :]
            weights[i, rows, :] = x
            larger = jnp.max(x.reshape(step // 8, 8, LANES), axis=0)
            top = larger if top is None else jnp.maximum(top, larger)
        total = jnp.zeros((8, LANES), jnp.float32)
        for at in range(0, ROWS, step):
            rows = pl.ds(at, step)
            e = jnp.exp(weights[i, rows, :].reshape(step // 8, 8, LANES) - top[None])
            weights[i, rows, :] = e.reshape(step, LANES)
            total += jnp.sum(e, axis=0)
        tops[i] = top
        larger = jnp.max(top, axis=0, keepdims=True)
        total = jnp.sum(total * jnp.exp(top - larger), axis=0, keepdims=True)
        lse[i : i + 1, :] = larger + jnp.log(total)


def row_kernel(weights, tops, got, send, potential, scale):
    larger = got[0]
    for d in range(1, N_PEERS):
        larger = jnp.maximum(larger, got[d])
    total = jnp.exp(got[0] - larger)
    for d in range(1, N_PEERS):
        total += jnp.exp(got[d] - larger)
    target = LOG_N - (larger + jnp.log(total))
    potential[...] = target
    for i in range(COL_BLOCKS):
        scale[i] = jnp.exp(tops[i] + target[i : i + 1, :])
    for b in range(ROW_BLOCKS):
        rows = pl.ds(b * LANES, LANES)
        total = jnp.zeros((LANES // 8, 8, LANES), jnp.float32)
        for i in range(COL_BLOCKS):
            total += weights[i, rows, :].reshape(LANES // 8, 8, LANES) * scale[i][None]
        total = jnp.transpose(total.reshape(LANES, LANES))
        total = jnp.sum(total, axis=0, keepdims=True)
        for d in range(N_TGT):
            send[d, b : b + 1, :] = total
            send[d, b + 4 : b + 5, :] = total


def last_kernel(weights, scale, got, before, sums, potential, factor):
    total = got[0, 0:4, :]
    for d in range(1, N_TGT):
        total += got[d, 0:4, :]
    source = before[0:4, :] + (LOG_N - jnp.log(total))
    potential[0:4, :] = source
    potential[4:8, :] = source
    ratio = 16384.0 / total
    for b in range(ROW_BLOCKS):
        factor[pl.ds(b * LANES, LANES), :] = spread(ratio[b : b + 1, :])

    step = 64
    for i in range(COL_BLOCKS):
        total = jnp.zeros((8, LANES), jnp.float32)
        for at in range(0, ROWS, step):
            rows = pl.ds(at, step)
            e = weights[i, rows, :] * factor[rows, :]
            total += jnp.sum(e.reshape(step // 8, 8, LANES), axis=0)
        total = jnp.sum(total * scale[i], axis=0, keepdims=True)
        for d in range(N_PEERS):
            sums[d, i : i + 1, :] = total


def call(kernel, outs, scratch, ins, cost=None, limit=VMEM_LIMIT):
    return pl.pallas_call(
        kernel,
        out_shape=[jax.ShapeDtypeStruct(shape, dtype) for shape, dtype in outs],
        in_specs=ins,
        out_specs=[VMEM() for _ in outs],
        scratch_shapes=scratch,
        cost_estimate=cost,
        compiler_params=pltpu.CompilerParams(vmem_limit_bytes=limit),
    )


def swap(value, axis, size, xor):
    return lax.ppermute(value, axis, [(i, i ^ xor) for i in range(size)])


def direct(value, axis):
    far, near, beyond = (swap(value, axis, 4, xor) for xor in (2, 1, 3))
    return [value, far, near, beyond]


def exchange(value, axes):
    return lax.all_to_all(value, axes, 0, 0)


def on_device(
    source_feats, source_tiles, source_links, target_feats, target_tiles, target_links,
    near_first, self_first, near_second, self_second,
):
    f32, bf16 = jnp.float32, jnp.bfloat16
    me = lax.axis_index(("zh", "x", "c"))
    me_source = lax.axis_index(("y", "zl"))

    held, source = pack(target_feats, target_tiles, target_links, source_feats, source_tiles, source_links)
    held, source, *weights = lax.optimization_barrier(
        (held, source, near_first, self_first, near_second, self_second)
    )
    weights = jnp.concatenate(weights, axis=0)
    source = jnp.concatenate([source, swap(source, "zl", 2, 1)], axis=0)
    held = jnp.concatenate(direct(held, "zh"), axis=0)
    held, source, weights = lax.optimization_barrier((held, source, weights))
    source = direct(source, "y")
    own = direct(held, "x")
    own[1:], source = lax.optimization_barrier((own[1:], source))
    other = [swap(piece, "c", 2, 1) for piece in own]
    own_links = jnp.concatenate([piece[:, 4 * PART, 0] for piece in own]).astype(jnp.int32)
    other_links = swap(own_links, "c", 2, 1)

    (emb_source,) = call(
        source_kernel,
        [((ROWS, D), bf16)],
        [pltpu.VMEM((ROWS, D), bf16)] * 3,
        [SMEM()] * 2 + [VMEM()] * 5,
        pl.CostEstimate(flops=700_000_000, bytes_accessed=2_000_000, transcendentals=0),
    )(
        me_source[None],
        jnp.concatenate([piece[:, 4 * PART, 0] for piece in source]).astype(jnp.int32),
        *source,
        weights,
    )

    scores, send = call(
        target_kernel,
        [((COL_BLOCKS, ROWS, LANES), f32), ((N_TGT, 8, LANES), f32)],
        [pltpu.VMEM((COLS, D), bf16)] * 4,
        [SMEM()] * 3 + [VMEM()] * 10,
    )(me[None], own_links, other_links, *own, *other, weights, emb_source)

    got = exchange(send, ("y", "zl"))
    spread_weights, tops, lse, source_first = call(
        column_kernel,
        [
            ((COL_BLOCKS, ROWS, LANES), f32),
            ((COL_BLOCKS, 8, LANES), f32),
            ((COL_BLOCKS, LANES), f32),
            ((8, LANES), f32),
        ],
        [pltpu.VMEM((ROWS, LANES), f32)],
        [VMEM()] * 2,
    )(scores, got)

    lse = jnp.logaddexp(lse, swap(lse, "c", 2, 1))
    got = exchange(jnp.broadcast_to(lse, (N_PEERS, COL_BLOCKS, LANES)), ("zh", "x"))
    send, target_first, scale = call(
        row_kernel,
        [((N_TGT, 8, LANES), f32), ((COL_BLOCKS, LANES), f32), ((COL_BLOCKS, 8, LANES), f32)],
        [],
        [VMEM()] * 3,
    )(spread_weights, tops, got)

    got = exchange(send, ("y", "zl"))
    sums, source_potential = call(
        last_kernel,
        [((N_PEERS, COL_BLOCKS, LANES), f32), ((8, LANES), f32)],
        [pltpu.VMEM((ROWS, LANES), f32)],
        [VMEM()] * 4,
    )(spread_weights, scale, got, source_first)

    total = jnp.sum(exchange(sums, ("zh", "x")), axis=0)
    total = total + swap(total, "c", 2, 1)
    target_potential = target_first + (LOG_N - jnp.log(total))
    return source_potential[0:4].reshape(ROWS), target_potential.reshape(COLS)


def solution(mesh):
    fine = Mesh(mesh.devices.reshape(4, 4, 2, 4, 2), ("zh", "x", "c", "y", "zl"))
    src, tgt = ("zh", "x", "c"), ("y", "zl")
    return jax.shard_map(
        on_device,
        mesh=fine,
        in_specs=(P(src, tgt, None),) * 3 + (P(tgt, src, None),) * 3 + (P(),) * 4,
        out_specs=(P(src), P(tgt)),
        check_vma=False,
    )
```

```python
import functools
import math

import jax
import jax.numpy as jnp
from jax import lax
from jax.experimental import pallas as pl
from jax.experimental.pallas import tpu as pltpu
from jax.sharding import Mesh, PartitionSpec as P

D = 384
PART = 64
PACK = 272
OWN_ROWS = 512
BLOCK = 2048
ROWS = 1024
COLS = 1024
LANES = 128
ROW_BLOCKS = ROWS // LANES
COL_BLOCKS = COLS // LANES
N_ROW_PEERS = 16
STEP = 512
N_PEERS = 16
LOG_N = math.log(16384.0)
VMEM_LIMIT = 32 * 1024 * 1024
PACK_LIMIT = 60 * 1024 * 1024

VMEM = functools.partial(pl.BlockSpec, memory_space=pltpu.VMEM)
HBM = functools.partial(pl.BlockSpec, memory_space=pltpu.HBM)
SMEM = functools.partial(pl.BlockSpec, memory_space=pltpu.SMEM)


def pack_kernel(*refs):
    sources, outs, held, sems = refs[:6], refs[6:8], refs[8:14], refs[14]
    copies = [pltpu.make_async_copy(src, dst, sems.at[i]) for i, (src, dst) in enumerate(zip(sources, held))]
    for copy in copies:
        copy.start()
    for graph, out in enumerate(outs):
        for copy in copies[3 * graph : 3 * graph + 3]:
            copy.wait()
        feats, tiles, links = held[3 * graph : 3 * graph + 3]
        for piece in range(D // LANES):
            out[0, piece * PART : (piece + 1) * PART, :] = feats[0, :, piece * LANES : (piece + 1) * LANES]
        out[0, 3 * PART : 4 * PART, :] = tiles[0]
        link = jnp.broadcast_to(links[0, 0:1, 1:2].astype(jnp.float32), (16, LANES))
        out[0, 4 * PART : PACK, :] = link.astype(jnp.bfloat16)


def pack(*arrays):
    return call(
        pack_kernel,
        [((1, PACK, LANES), jnp.bfloat16)] * 2,
        [pltpu.VMEM(v.shape, v.dtype) for v in arrays] + [pltpu.SemaphoreType.DMA((6,))],
        [HBM()] * 6,
        limit=PACK_LIMIT,
    )(*arrays)


def graph_layers(packed, first, second, weights, x_ref, s_ref, h_ref, emit, wanted):
    count = x_ref.shape[0] // PART
    for k in range(count):
        ref, at = packed(k)
        for piece in range(D // LANES):
            x_ref[k * PART : (k + 1) * PART, piece * LANES : (piece + 1) * LANES] = ref[
                at, piece * PART : (piece + 1) * PART, :
            ]

    def neighbour_sums(src, count):
        for k in range(count):
            ref, at = packed(k)
            near = src[pl.ds(first(k) * PART, PART), :]
            other = src[pl.ds(pl.multiple_of(second(k) * PART, PART), PART), :]
            panel = ref[at, 3 * PART : 4 * PART, :]
            both = jnp.concatenate([near, other], axis=0)
            total = jnp.dot(panel, both, preferred_element_type=jnp.float32)
            s_ref[k * PART : (k + 1) * PART, :] = total.astype(jnp.bfloat16)

    def mix(src, at, layer):
        left = jnp.concatenate([s_ref[at : at + STEP, :], src[at : at + STEP, :]], axis=1)
        right = weights[layer * 2 * D : (layer + 1) * 2 * D, :]
        return jnp.dot(left, right, preferred_element_type=jnp.float32)

    neighbour_sums(x_ref, count)
    for at in range(0, count * PART, STEP):
        h_ref[at : at + STEP, :] = jnp.maximum(mix(x_ref, at, 0), 0.0).astype(jnp.bfloat16)
    neighbour_sums(h_ref, wanted)
    for at in range(0, wanted * PART, STEP):
        emit(at, mix(h_ref, at, 1).astype(jnp.bfloat16))


def turn(v):
    return ((v & 1) << 1) | (v >> 1)


def slot_xor(k):
    return (turn(k & 3) << 3) | (turn((k >> 2) & 3) << 1) | (k >> 4)


def slot_of(v):
    return turn(v >> 3) | (turn((v >> 1) & 3) << 2) | ((v & 1) << 4)


def source_kernel(place, links, own0, own1, own2, own3, weights, out, x_ref, s_ref, h_ref):
    me = place[0]
    pieces = (own0, own1, own2, own3)

    def emit(at, value):
        for k in range(value.shape[0] // PART):
            slot = at // PART + k
            q = me ^ ((turn(slot >> 1) << 1) | (slot & 1))
            out[pl.ds(pl.multiple_of(q * PART, PART), PART), :] = value[k * PART : (k + 1) * PART, :]

    graph_layers(
        lambda k: (pieces[k // 2], k % 2),
        lambda k: k ^ 7,
        lambda k: (turn((links[k] ^ me) >> 1) << 1) | ((links[k] ^ me) & 1),
        weights, x_ref, s_ref, h_ref, emit, 8,
    )


def spread(row):
    return jnp.transpose(jnp.broadcast_to(row, (LANES, LANES)))


def target_kernel(
    place, own_links, other_links,
    own0, own1, own2, own3, other0, other1, other2, other3,
    weights,
    out, x_ref, s_ref, h_ref,
):
    me = place[0]
    pieces = (own0, own1, own2, own3, other0, other1, other2, other3)

    def emit(at, value):
        for piece in range(value.shape[0] // PART):
            i = (me ^ slot_xor(at // PART + piece)) >> 1
            row = (i & 7) * LANES + (i >> 3) * PART
            out[pl.ds(pl.multiple_of(row, PART), PART), :] = value[piece * PART : (piece + 1) * PART, :]

    graph_layers(
        lambda k: (pieces[k // 4], k % 4),
        lambda k: k ^ 31,
        lambda k: slot_of((own_links[k] if k < 16 else other_links[k - 16]) ^ me),
        weights, x_ref, s_ref, h_ref, emit, 16,
    )


def score_kernel(place, own_source, other_source, emb_target, scores, send, e_ref):
    core = place[0] & 1
    e_ref[pl.ds(pl.multiple_of(core * OWN_ROWS, OWN_ROWS), OWN_ROWS), :] = own_source[...]
    e_ref[pl.ds(pl.multiple_of((1 - core) * OWN_ROWS, OWN_ROWS), OWN_ROWS), :] = other_source[...]
    for at in range(0, ROWS, 256):
        rows = pl.ds(at, 256)
        top = None
        for i in range(COL_BLOCKS // 2):
            part = lax.dot_general(
                e_ref[rows, :],
                emb_target[i * 256 : (i + 1) * 256, :],
                (((1,), (1,)), ((), ())),
                preferred_element_type=jnp.float32,
            )
            part = 0.2 * part
            scores[2 * i, rows, :] = part[:, :LANES]
            scores[2 * i + 1, rows, :] = part[:, LANES:]
            larger = jnp.maximum(part[:, :LANES], part[:, LANES:])
            top = larger if top is None else jnp.maximum(top, larger)
        total = jnp.exp(scores[0, rows, :] - top)
        for i in range(1, COL_BLOCKS):
            total += jnp.exp(scores[i, rows, :] - top)
        for half in range(2):
            b = at // LANES + half
            part_top = jnp.transpose(top[half * LANES : (half + 1) * LANES])
            part_total = jnp.transpose(total[half * LANES : (half + 1) * LANES])
            larger = jnp.max(part_top, axis=0, keepdims=True)
            part_total = jnp.sum(part_total * jnp.exp(part_top - larger), axis=0, keepdims=True)
            for d in range(N_ROW_PEERS):
                send[d, b : b + 1, :] = larger
                send[d, ROW_BLOCKS + b : ROW_BLOCKS + b + 1, :] = part_total


def column_kernel(scores, got, weights, tops, send, potential, shift):
    top, total = got[0, 0:ROW_BLOCKS, :], got[0, ROW_BLOCKS:, :]
    larger = top
    for d in range(1, N_ROW_PEERS):
        larger = jnp.maximum(larger, got[d, 0:ROW_BLOCKS, :])
    total = total * jnp.exp(top - larger)
    for d in range(1, N_ROW_PEERS):
        total += got[d, ROW_BLOCKS:, :] * jnp.exp(got[d, 0:ROW_BLOCKS, :] - larger)
    source = LOG_N - (larger + jnp.log(total))
    potential[...] = source
    for b in range(ROW_BLOCKS):
        shift[pl.ds(b * LANES, LANES), :] = spread(source[b : b + 1, :])

    step = 64
    for i in range(COL_BLOCKS):
        top = None
        for at in range(0, ROWS, step):
            rows = pl.ds(at, step)
            x = scores[i, rows, :] + shift[rows, :]
            weights[i, rows, :] = x
            larger = jnp.max(x.reshape(step // 8, 8, LANES), axis=0)
            top = larger if top is None else jnp.maximum(top, larger)
        total = jnp.zeros((8, LANES), jnp.float32)
        for at in range(0, ROWS, step):
            rows = pl.ds(at, step)
            e = jnp.exp(weights[i, rows, :].reshape(step // 8, 8, LANES) - top[None])
            weights[i, rows, :] = e.reshape(step, LANES)
            total += jnp.sum(e, axis=0)
        tops[i] = top
        larger = jnp.max(top, axis=0, keepdims=True)
        total = jnp.sum(total * jnp.exp(top - larger), axis=0, keepdims=True)
        total = larger + jnp.log(total)
        for d in range(N_PEERS):
            send[d, i : i + 1, :] = total


def row_kernel(weights, tops, got, send, potential, scale):
    larger = got[0]
    for d in range(1, N_PEERS):
        larger = jnp.maximum(larger, got[d])
    total = jnp.exp(got[0] - larger)
    for d in range(1, N_PEERS):
        total += jnp.exp(got[d] - larger)
    target = LOG_N - (larger + jnp.log(total))
    potential[...] = target
    for i in range(COL_BLOCKS):
        scale[i] = jnp.exp(tops[i] + target[i : i + 1, :])
    for b in range(ROW_BLOCKS):
        rows = pl.ds(b * LANES, LANES)
        total = jnp.zeros((LANES // 8, 8, LANES), jnp.float32)
        for i in range(COL_BLOCKS):
            total += weights[i, rows, :].reshape(LANES // 8, 8, LANES) * scale[i][None]
        total = jnp.transpose(total.reshape(LANES, LANES))
        total = jnp.sum(total, axis=0, keepdims=True)
        for d in range(N_ROW_PEERS):
            send[d, b : b + 1, :] = total


def last_kernel(weights, scale, got, before, sums, potential, factor):
    total = got[0]
    for d in range(1, N_ROW_PEERS):
        total += got[d]
    potential[...] = before[...] + (LOG_N - jnp.log(total))
    ratio = 16384.0 / total
    for b in range(ROW_BLOCKS):
        factor[pl.ds(b * LANES, LANES), :] = spread(ratio[b : b + 1, :])

    step = 64
    for i in range(COL_BLOCKS):
        total = jnp.zeros((8, LANES), jnp.float32)
        for at in range(0, ROWS, step):
            rows = pl.ds(at, step)
            e = weights[i, rows, :] * factor[rows, :]
            total += jnp.sum(e.reshape(step // 8, 8, LANES), axis=0)
        total = jnp.sum(total * scale[i], axis=0, keepdims=True)
        for d in range(N_PEERS):
            sums[d, i : i + 1, :] = total


def call(kernel, outs, scratch, ins, cost=None, limit=VMEM_LIMIT):
    return pl.pallas_call(
        kernel,
        out_shape=[jax.ShapeDtypeStruct(shape, dtype) for shape, dtype in outs],
        in_specs=ins,
        out_specs=[VMEM() for _ in outs],
        scratch_shapes=scratch,
        cost_estimate=cost,
        compiler_params=pltpu.CompilerParams(vmem_limit_bytes=limit),
    )


def swap(value, axis, size, xor):
    return lax.ppermute(value, axis, [(i, i ^ xor) for i in range(size)])


def direct(value, axis):
    far, near, beyond = (swap(value, axis, 4, xor) for xor in (2, 1, 3))
    return [value, far, near, beyond]


def exchange(value, axes):
    return lax.all_to_all(value, axes, 0, 0)


def on_device(
    source_feats, source_tiles, source_links, target_feats, target_tiles, target_links,
    near_first, self_first, near_second, self_second,
):
    f32, bf16 = jnp.float32, jnp.bfloat16
    me = lax.axis_index(("zh", "x", "c"))
    me_source = lax.axis_index(("y", "zl"))

    held, source = pack(target_feats, target_tiles, target_links, source_feats, source_tiles, source_links)
    held, source, *weights = lax.optimization_barrier(
        (held, source, near_first, self_first, near_second, self_second)
    )
    weights = jnp.concatenate(weights, axis=0)
    source = jnp.concatenate([source, swap(source, "zl", 2, 1)], axis=0)
    held = jnp.concatenate(direct(held, "zh"), axis=0)
    held, source, weights = lax.optimization_barrier((held, source, weights))
    source = direct(source, "y")
    own = direct(held, "x")
    own[1:], source = lax.optimization_barrier((own[1:], source))
    other = [swap(piece, "c", 2, 1) for piece in own]
    own_links = jnp.concatenate([piece[:, 4 * PART, 0] for piece in own]).astype(jnp.int32)
    other_links = swap(own_links, "c", 2, 1)

    (emb_source,) = call(
        source_kernel,
        [((OWN_ROWS, D), bf16)],
        [pltpu.VMEM((OWN_ROWS, D), bf16)] * 3,
        [SMEM()] * 2 + [VMEM()] * 5,
        pl.CostEstimate(flops=700_000_000, bytes_accessed=2_000_000, transcendentals=0),
    )(
        me_source[None],
        jnp.concatenate([piece[:, 4 * PART, 0] for piece in source]).astype(jnp.int32),
        *source,
        weights,
    )
    other_source = swap(emb_source, "c", 2, 1)

    (emb_target,) = call(
        target_kernel,
        [((COLS, D), bf16)],
        [pltpu.VMEM((BLOCK, D), bf16)] * 3,
        [SMEM()] * 3 + [VMEM()] * 9,
        pl.CostEstimate(flops=2_400_000_000, bytes_accessed=4_000_000, transcendentals=0),
    )(me[None], own_links, other_links, *own, *other, weights)

    scores, send = call(
        score_kernel,
        [((COL_BLOCKS, ROWS, LANES), f32), ((N_ROW_PEERS, 2 * ROW_BLOCKS, LANES), f32)],
        [pltpu.VMEM((ROWS, D), bf16)],
        [SMEM()] + [VMEM()] * 3,
    )(me[None], emb_source, other_source, emb_target)

    got = exchange(send, ("c", "y", "zl"))
    spread_weights, tops, send, source_first = call(
        column_kernel,
        [
            ((COL_BLOCKS, ROWS, LANES), f32),
            ((COL_BLOCKS, 8, LANES), f32),
            ((N_PEERS, COL_BLOCKS, LANES), f32),
            ((ROW_BLOCKS, LANES), f32),
        ],
        [pltpu.VMEM((ROWS, LANES), f32)],
        [VMEM()] * 2,
    )(scores, got)

    got = exchange(send, ("zh", "x"))
    send, target_first, scale = call(
        row_kernel,
        [((N_ROW_PEERS, ROW_BLOCKS, LANES), f32), ((COL_BLOCKS, LANES), f32), ((COL_BLOCKS, 8, LANES), f32)],
        [],
        [VMEM()] * 3,
    )(spread_weights, tops, got)

    got = exchange(send, ("c", "y", "zl"))
    sums, source_potential = call(
        last_kernel,
        [((N_PEERS, COL_BLOCKS, LANES), f32), ((ROW_BLOCKS, LANES), f32)],
        [pltpu.VMEM((ROWS, LANES), f32)],
        [VMEM()] * 4,
    )(spread_weights, scale, got, source_first)

    total = jnp.sum(exchange(sums, ("zh", "x")), axis=0)
    half = target_first + (LOG_N - jnp.log(total))
    other_half = swap(half, "c", 2, 1)
    first = (me & 1) == 0
    even, odd = jnp.where(first, half, other_half), jnp.where(first, other_half, half)
    target_potential = jnp.concatenate(
        [jnp.concatenate([v[:, at : at + PART] for v in (even, odd)], axis=1) for at in (0, PART)], axis=0
    )
    rows = ROW_BLOCKS // 2
    source_potential = jnp.where(first, source_potential[:rows], source_potential[rows:])
    return source_potential.reshape(OWN_ROWS), target_potential.reshape(BLOCK)


def solution(mesh):
    fine = Mesh(mesh.devices.reshape(4, 4, 2, 4, 2), ("zh", "x", "c", "y", "zl"))
    src, tgt = ("zh", "x", "c"), ("y", "zl")
    return jax.shard_map(
        on_device,
        mesh=fine,
        in_specs=(P(src, tgt, None),) * 3 + (P(tgt, src, None),) * 3 + (P(),) * 4,
        out_specs=(P(src), P(tgt)),
        check_vma=False,
    )
```

```python
import functools
import math

import jax
import jax.numpy as jnp
from jax import lax
from jax.experimental import pallas as pl
from jax.experimental.pallas import tpu as pltpu
from jax.sharding import Mesh, PartitionSpec as P

D = 384
PART = 64
PACK = 272
OWN_ROWS = 512
BLOCK = 2048
ROWS = 1024
COLS = 1024
LANES = 128
ROW_BLOCKS = ROWS // LANES
COL_BLOCKS = COLS // LANES
N_ROW_PEERS = 16
STEP = 512
N_PEERS = 16
LOG_N = math.log(16384.0)
VMEM_LIMIT = 18 * 1024 * 1024
PACK_LIMIT = 60 * 1024 * 1024

VMEM = functools.partial(pl.BlockSpec, memory_space=pltpu.VMEM)
HBM = functools.partial(pl.BlockSpec, memory_space=pltpu.HBM)
SMEM = functools.partial(pl.BlockSpec, memory_space=pltpu.SMEM)


def pack_kernel(*refs):
    sources, outs, held, sems = refs[:6], refs[6:8], refs[8:14], refs[14]
    copies = [pltpu.make_async_copy(src, dst, sems.at[i]) for i, (src, dst) in enumerate(zip(sources, held))]
    for copy in copies:
        copy.start()
    for graph, out in enumerate(outs):
        for copy in copies[3 * graph : 3 * graph + 3]:
            copy.wait()
        feats, tiles, links = held[3 * graph : 3 * graph + 3]
        for piece in range(D // LANES):
            out[0, piece * PART : (piece + 1) * PART, :] = feats[0, :, piece * LANES : (piece + 1) * LANES]
        out[0, 3 * PART : 4 * PART, :] = tiles[0]
        link = jnp.broadcast_to(links[0, 0:1, 1:2].astype(jnp.float32), (16, LANES))
        out[0, 4 * PART : PACK, :] = link.astype(jnp.bfloat16)


def pack(*arrays):
    return call(
        pack_kernel,
        [((1, PACK, LANES), jnp.bfloat16)] * 2,
        [pltpu.VMEM(v.shape, v.dtype) for v in arrays] + [pltpu.SemaphoreType.DMA((6,))],
        [HBM()] * 6,
        limit=PACK_LIMIT,
    )(*arrays)


def graph_layers(packed, first, second, weights, x_ref, s_ref, h_ref, row_ref, link_ref, sem, emit, wanted):
    count = x_ref.shape[0] // PART
    lane = lax.broadcasted_iota(jnp.int32, (8, LANES), 1)
    row = jnp.zeros((8, LANES), jnp.int32)
    for k in range(count):
        ref, at = packed(k)
        link = ref[at, 4 * PART : PACK, :].astype(jnp.float32)[0:8]
        row = jnp.where(lane == k, link.astype(jnp.int32), row)
    row_ref[...] = row
    copy = pltpu.make_async_copy(row_ref, link_ref, sem)
    copy.start()
    for k in range(count):
        ref, at = packed(k)
        for piece in range(D // LANES):
            x_ref[k * PART : (k + 1) * PART, piece * LANES : (piece + 1) * LANES] = ref[
                at, piece * PART : (piece + 1) * PART, :
            ]
    copy.wait()

    def neighbour_sums(src, count):
        for k in range(count):
            ref, at = packed(k)
            near = src[pl.ds(first(k) * PART, PART), :]
            other = src[pl.ds(pl.multiple_of(second(link_ref[0, k]) * PART, PART), PART), :]
            panel = ref[at, 3 * PART : 4 * PART, :]
            both = jnp.concatenate([near, other], axis=0)
            total = jnp.dot(panel, both, preferred_element_type=jnp.float32)
            s_ref[k * PART : (k + 1) * PART, :] = total.astype(jnp.bfloat16)

    def mix(src, at, layer):
        left = jnp.concatenate([s_ref[at : at + STEP, :], src[at : at + STEP, :]], axis=1)
        right = weights[layer * 2 * D : (layer + 1) * 2 * D, :]
        return jnp.dot(left, right, preferred_element_type=jnp.float32)

    neighbour_sums(x_ref, count)
    for at in range(0, count * PART, STEP):
        h_ref[at : at + STEP, :] = jnp.maximum(mix(x_ref, at, 0), 0.0).astype(jnp.bfloat16)
    neighbour_sums(h_ref, wanted)
    for at in range(0, wanted * PART, STEP):
        emit(at, mix(h_ref, at, 1).astype(jnp.bfloat16))


def turn(v):
    return ((v & 1) << 1) | (v >> 1)


def slot_xor(k):
    return (turn(k & 3) << 3) | (turn((k >> 2) & 3) << 1) | (k >> 4)


def slot_of(v):
    return turn(v >> 3) | (turn((v >> 1) & 3) << 2) | ((v & 1) << 4)


def source_kernel(place, own0, own1, own2, own3, weights, out, *scratch):
    me = place[0]
    pieces = (own0, own1, own2, own3)

    def emit(at, value):
        for k in range(value.shape[0] // PART):
            slot = at // PART + k
            q = me ^ ((turn(slot >> 1) << 1) | (slot & 1))
            out[pl.ds(pl.multiple_of(q * PART, PART), PART), :] = value[k * PART : (k + 1) * PART, :]

    graph_layers(
        lambda k: (pieces[k // 2], k % 2),
        lambda k: k ^ 7,
        lambda link: (turn((link ^ me) >> 1) << 1) | ((link ^ me) & 1),
        weights, *scratch, emit, 8,
    )


def spread(row):
    return jnp.transpose(jnp.broadcast_to(row, (LANES, LANES)))


def target_kernel(
    place, own0, own1, own2, own3, other0, other1, other2, other3, weights, out, *scratch
):
    me = place[0]
    pieces = (own0, own1, own2, own3, other0, other1, other2, other3)

    def emit(at, value):
        for piece in range(value.shape[0] // PART):
            i = (me ^ slot_xor(at // PART + piece)) >> 1
            row = (i & 7) * LANES + (i >> 3) * PART
            out[pl.ds(pl.multiple_of(row, PART), PART), :] = value[piece * PART : (piece + 1) * PART, :]

    graph_layers(
        lambda k: (pieces[k // 4], k % 4),
        lambda k: k ^ 31,
        lambda link: slot_of(link ^ me),
        weights, *scratch, emit, 16,
    )


def score_kernel(place, own_source, other_source, emb_target, scores, send, e_ref):
    core = place[0] & 1
    e_ref[pl.ds(pl.multiple_of(core * OWN_ROWS, OWN_ROWS), OWN_ROWS), :] = own_source[...]
    e_ref[pl.ds(pl.multiple_of((1 - core) * OWN_ROWS, OWN_ROWS), OWN_ROWS), :] = other_source[...]
    for at in range(0, ROWS, 256):
        rows = pl.ds(at, 256)
        top = None
        for i in range(COL_BLOCKS // 2):
            part = lax.dot_general(
                e_ref[rows, :],
                emb_target[i * 256 : (i + 1) * 256, :],
                (((1,), (1,)), ((), ())),
                preferred_element_type=jnp.float32,
            )
            part = 0.2 * part
            scores[2 * i, rows, :] = part[:, :LANES]
            scores[2 * i + 1, rows, :] = part[:, LANES:]
            larger = jnp.maximum(part[:, :LANES], part[:, LANES:])
            top = larger if top is None else jnp.maximum(top, larger)
        total = jnp.exp(scores[0, rows, :] - top)
        for i in range(1, COL_BLOCKS):
            total += jnp.exp(scores[i, rows, :] - top)
        for half in range(2):
            b = at // LANES + half
            part_top = jnp.transpose(top[half * LANES : (half + 1) * LANES])
            part_total = jnp.transpose(total[half * LANES : (half + 1) * LANES])
            larger = jnp.max(part_top, axis=0, keepdims=True)
            part_total = jnp.sum(part_total * jnp.exp(part_top - larger), axis=0, keepdims=True)
            for d in range(N_ROW_PEERS):
                send[d, b : b + 1, :] = larger
                send[d, ROW_BLOCKS + b : ROW_BLOCKS + b + 1, :] = part_total


def column_kernel(scores, got, weights, tops, send, potential):
    top, total = got[0, 0:ROW_BLOCKS, :], got[0, ROW_BLOCKS:, :]
    larger = top
    for d in range(1, N_ROW_PEERS):
        larger = jnp.maximum(larger, got[d, 0:ROW_BLOCKS, :])
    total = total * jnp.exp(top - larger)
    for d in range(1, N_ROW_PEERS):
        total += got[d, ROW_BLOCKS:, :] * jnp.exp(got[d, 0:ROW_BLOCKS, :] - larger)
    source = LOG_N - (larger + jnp.log(total))
    potential[...] = source
    peaks = [None] * COL_BLOCKS
    for b in range(ROW_BLOCKS):
        rows = pl.ds(b * LANES, LANES)
        shift = spread(source[b : b + 1, :])
        for i in range(COL_BLOCKS):
            x = scores[i, rows, :] + shift
            weights[i, rows, :] = x
            peak = jnp.max(x.reshape(LANES // 8, 8, LANES), axis=0)
            peaks[i] = peak if b == 0 else jnp.maximum(peaks[i], peak)
    step = 64
    for i in range(COL_BLOCKS):
        top = peaks[i]
        total = jnp.zeros((8, LANES), jnp.float32)
        for at in range(0, ROWS, step):
            rows = pl.ds(at, step)
            e = jnp.exp(weights[i, rows, :].reshape(step // 8, 8, LANES) - top[None])
            weights[i, rows, :] = e.reshape(step, LANES)
            total += jnp.sum(e, axis=0)
        tops[i] = top
        larger = jnp.max(top, axis=0, keepdims=True)
        total = jnp.sum(total * jnp.exp(top - larger), axis=0, keepdims=True)
        total = larger + jnp.log(total)
        for d in range(N_PEERS):
            send[d, i : i + 1, :] = total


def row_kernel(weights, tops, got, send, potential, scale):
    larger = got[0]
    for d in range(1, N_PEERS):
        larger = jnp.maximum(larger, got[d])
    total = jnp.exp(got[0] - larger)
    for d in range(1, N_PEERS):
        total += jnp.exp(got[d] - larger)
    target = LOG_N - (larger + jnp.log(total))
    potential[...] = target
    for i in range(COL_BLOCKS):
        scale[i] = jnp.exp(tops[i] + target[i : i + 1, :])
    for b in range(ROW_BLOCKS):
        rows = pl.ds(b * LANES, LANES)
        total = jnp.zeros((LANES // 8, 8, LANES), jnp.float32)
        for i in range(COL_BLOCKS):
            total += weights[i, rows, :].reshape(LANES // 8, 8, LANES) * scale[i][None]
        total = jnp.transpose(total.reshape(LANES, LANES))
        total = jnp.sum(total, axis=0, keepdims=True)
        for d in range(N_ROW_PEERS):
            send[d, b : b + 1, :] = total


def last_kernel(weights, scale, got, before, sums, potential):
    total = got[0]
    for d in range(1, N_ROW_PEERS):
        total += got[d]
    potential[...] = before[...] + (LOG_N - jnp.log(total))
    ratio = 16384.0 / total
    parts = [jnp.zeros((8, LANES), jnp.float32)] * COL_BLOCKS
    for b in range(ROW_BLOCKS):
        rows = pl.ds(b * LANES, LANES)
        factor = spread(ratio[b : b + 1, :])
        for i in range(COL_BLOCKS):
            e = (weights[i, rows, :] * factor).reshape(LANES // 8, 8, LANES)
            parts[i] += jnp.sum(e, axis=0)
    for i in range(COL_BLOCKS):
        total = jnp.sum(parts[i] * scale[i], axis=0, keepdims=True)
        for d in range(N_PEERS):
            sums[d, i : i + 1, :] = total


def call(kernel, outs, scratch, ins, cost=None, limit=VMEM_LIMIT):
    return pl.pallas_call(
        kernel,
        out_shape=[jax.ShapeDtypeStruct(shape, dtype) for shape, dtype in outs],
        in_specs=ins,
        out_specs=[VMEM() for _ in outs],
        scratch_shapes=scratch,
        cost_estimate=cost,
        compiler_params=pltpu.CompilerParams(vmem_limit_bytes=limit),
    )


def graph_scratch(rows):
    return [pltpu.VMEM((rows, D), jnp.bfloat16)] * 3 + [
        pltpu.VMEM((8, LANES), jnp.int32),
        pltpu.SMEM((8, LANES), jnp.int32),
        pltpu.SemaphoreType.DMA,
    ]


def swap(value, axis, size, xor):
    return lax.ppermute(value, axis, [(i, i ^ xor) for i in range(size)])


def direct(value, axis):
    far, near, beyond = (swap(value, axis, 4, xor) for xor in (2, 1, 3))
    return [value, far, near, beyond]


def exchange(value, axes):
    return lax.all_to_all(value, axes, 0, 0)


def on_device(
    source_feats, source_tiles, source_links, target_feats, target_tiles, target_links,
    near_first, self_first, near_second, self_second,
):
    f32, bf16 = jnp.float32, jnp.bfloat16
    me = lax.axis_index(("zh", "x", "c"))
    me_source = lax.axis_index(("y", "zl"))

    held, source = pack(target_feats, target_tiles, target_links, source_feats, source_tiles, source_links)
    held, source, *weights = lax.optimization_barrier(
        (held, source, near_first, self_first, near_second, self_second)
    )
    weights = jnp.concatenate(weights, axis=0)
    source = jnp.concatenate([source, swap(source, "zl", 2, 1)], axis=0)
    held = jnp.concatenate(direct(held, "zh"), axis=0)
    held, source, weights = lax.optimization_barrier((held, source, weights))
    source = direct(source, "y")
    own = direct(held, "x")
    own[1:], source = lax.optimization_barrier((own[1:], source))
    other = [swap(piece, "c", 2, 1) for piece in own]

    (emb_source,) = call(
        source_kernel,
        [((OWN_ROWS, D), bf16)],
        graph_scratch(OWN_ROWS),
        [SMEM()] + [VMEM()] * 5,
        pl.CostEstimate(flops=700_000_000, bytes_accessed=2_000_000, transcendentals=0),
    )(
        me_source[None],
        *source,
        weights,
    )
    other_source = swap(emb_source, "c", 2, 1)

    (emb_target,) = call(
        target_kernel,
        [((COLS, D), bf16)],
        graph_scratch(BLOCK),
        [SMEM()] + [VMEM()] * 9,
        pl.CostEstimate(flops=2_400_000_000, bytes_accessed=4_000_000, transcendentals=0),
    )(me[None], *own, *other, weights)

    scores, send = call(
        score_kernel,
        [((COL_BLOCKS, ROWS, LANES), f32), ((N_ROW_PEERS, 2 * ROW_BLOCKS, LANES), f32)],
        [pltpu.VMEM((ROWS, D), bf16)],
        [SMEM()] + [VMEM()] * 3,
    )(me[None], emb_source, other_source, emb_target)

    got = exchange(send, ("c", "y", "zl"))
    spread_weights, tops, send, source_first = call(
        column_kernel,
        [
            ((COL_BLOCKS, ROWS, LANES), f32),
            ((COL_BLOCKS, 8, LANES), f32),
            ((N_PEERS, COL_BLOCKS, LANES), f32),
            ((ROW_BLOCKS, LANES), f32),
        ],
        [],
        [VMEM()] * 2,
    )(scores, got)

    got = exchange(send, ("zh", "x"))
    send, target_first, scale = call(
        row_kernel,
        [((N_ROW_PEERS, ROW_BLOCKS, LANES), f32), ((COL_BLOCKS, LANES), f32), ((COL_BLOCKS, 8, LANES), f32)],
        [],
        [VMEM()] * 3,
    )(spread_weights, tops, got)

    got = exchange(send, ("c", "y", "zl"))
    sums, source_potential = call(
        last_kernel,
        [((N_PEERS, COL_BLOCKS, LANES), f32), ((ROW_BLOCKS, LANES), f32)],
        [],
        [VMEM()] * 4,
    )(spread_weights, scale, got, source_first)

    total = jnp.sum(exchange(sums, ("zh", "x")), axis=0)
    half = target_first + (LOG_N - jnp.log(total))
    other_half = swap(half, "c", 2, 1)
    first = (me & 1) == 0
    even, odd = jnp.where(first, half, other_half), jnp.where(first, other_half, half)
    target_potential = jnp.concatenate(
        [jnp.concatenate([v[:, at : at + PART] for v in (even, odd)], axis=1) for at in (0, PART)], axis=0
    )
    rows = ROW_BLOCKS // 2
    source_potential = jnp.where(first, source_potential[:rows], source_potential[rows:])
    return source_potential.reshape(OWN_ROWS), target_potential.reshape(BLOCK)


def solution(mesh):
    fine = Mesh(mesh.devices.reshape(4, 4, 2, 4, 2), ("zh", "x", "c", "y", "zl"))
    src, tgt = ("zh", "x", "c"), ("y", "zl")
    return jax.shard_map(
        on_device,
        mesh=fine,
        in_specs=(P(src, tgt, None),) * 3 + (P(tgt, src, None),) * 3 + (P(),) * 4,
        out_specs=(P(src), P(tgt)),
        check_vma=False,
    )
```

```python
import functools
import math

import jax
import jax.numpy as jnp
from jax import lax
from jax.experimental import pallas as pl
from jax.experimental.pallas import tpu as pltpu
from jax.sharding import Mesh, PartitionSpec as P

D = 384
PART = 64
PACK = 272
OWN_ROWS = 512
BLOCK = 2048
ROWS = 1024
COLS = 1024
LANES = 128
ROW_BLOCKS = ROWS // LANES
COL_BLOCKS = COLS // LANES
N_ROW_PEERS = 16
STEP = 512
N_PEERS = 16
LOG_N = math.log(16384.0)
VMEM_LIMIT = 18 * 1024 * 1024
PACK_LIMIT = 60 * 1024 * 1024

VMEM = functools.partial(pl.BlockSpec, memory_space=pltpu.VMEM)
HBM = functools.partial(pl.BlockSpec, memory_space=pltpu.HBM)
SMEM = functools.partial(pl.BlockSpec, memory_space=pltpu.SMEM)


def pack_kernel(*refs):
    sources, outs, held, sems = refs[:6], refs[6:8], refs[8:14], refs[14]
    copies = [pltpu.make_async_copy(src, dst, sems.at[i]) for i, (src, dst) in enumerate(zip(sources, held))]
    for copy in copies:
        copy.start()
    for graph, out in enumerate(outs):
        for copy in copies[3 * graph : 3 * graph + 3]:
            copy.wait()
        feats, tiles, links = held[3 * graph : 3 * graph + 3]
        for piece in range(D // LANES):
            out[0, piece * PART : (piece + 1) * PART, :] = feats[0, :, piece * LANES : (piece + 1) * LANES]
        out[0, 3 * PART : 4 * PART, :] = tiles[0]
        link = jnp.broadcast_to(links[0, 0:1, 1:2].astype(jnp.float32), (16, LANES))
        out[0, 4 * PART : PACK, :] = link.astype(jnp.bfloat16)


def pack(*arrays):
    return call(
        pack_kernel,
        [((1, PACK, LANES), jnp.bfloat16)] * 2,
        [pltpu.VMEM(v.shape, v.dtype) for v in arrays] + [pltpu.SemaphoreType.DMA((6,))],
        [HBM()] * 6,
        limit=PACK_LIMIT,
    )(*arrays)


def graph_layers(packed, first, second, weights, x_ref, s_ref, h_ref, row_ref, link_ref, sem, emit, wanted):
    count = x_ref.shape[0] // PART
    lane = lax.broadcasted_iota(jnp.int32, (8, LANES), 1)
    row = jnp.zeros((8, LANES), jnp.int32)
    for k in range(count):
        ref, at = packed(k)
        link = ref[at, 4 * PART : PACK, :].astype(jnp.float32)[0:8]
        row = jnp.where(lane == k, link.astype(jnp.int32), row)
    row_ref[...] = row
    copy = pltpu.make_async_copy(row_ref, link_ref, sem)
    copy.start()
    for k in range(count):
        ref, at = packed(k)
        for piece in range(D // LANES):
            x_ref[k * PART : (k + 1) * PART, piece * LANES : (piece + 1) * LANES] = ref[
                at, piece * PART : (piece + 1) * PART, :
            ]
    copy.wait()

    def neighbour_sums(src, count):
        for k in range(count):
            ref, at = packed(k)
            near = src[pl.ds(first(k) * PART, PART), :]
            other = src[pl.ds(pl.multiple_of(second(link_ref[0, k]) * PART, PART), PART), :]
            panel = ref[at, 3 * PART : 4 * PART, :]
            both = jnp.concatenate([near, other], axis=0)
            total = jnp.dot(panel, both, preferred_element_type=jnp.float32)
            s_ref[k * PART : (k + 1) * PART, :] = total.astype(jnp.bfloat16)

    def mix(src, at, layer):
        left = jnp.concatenate([s_ref[at : at + STEP, :], src[at : at + STEP, :]], axis=1)
        right = weights[layer * 2 * D : (layer + 1) * 2 * D, :]
        return jnp.dot(left, right, preferred_element_type=jnp.float32)

    neighbour_sums(x_ref, count)
    for at in range(0, count * PART, STEP):
        h_ref[at : at + STEP, :] = jnp.maximum(mix(x_ref, at, 0), 0.0).astype(jnp.bfloat16)
    neighbour_sums(h_ref, wanted)
    for at in range(0, wanted * PART, STEP):
        emit(at, mix(h_ref, at, 1).astype(jnp.bfloat16))


def turn(v):
    return v ^ (v >> 1)


def slot_xor(k):
    return (turn(k & 3) << 3) | (turn((k >> 2) & 3) << 1) | (k >> 4)


def slot_of(v):
    return turn(v >> 3) | (turn((v >> 1) & 3) << 2) | ((v & 1) << 4)


def source_xor(k):
    return (turn(k >> 1) << 1) | (k & 1)


source_of = source_xor


def source_kernel(place, packed, weights, out, *scratch):
    me = place[0]

    def emit(at, value):
        for k in range(value.shape[0] // PART):
            q = me ^ source_xor(at // PART + k)
            out[pl.ds(pl.multiple_of(q * PART, PART), PART), :] = value[k * PART : (k + 1) * PART, :]

    graph_layers(
        lambda k: (packed, k),
        lambda k: k ^ source_of(7),
        lambda link: source_of(link ^ me),
        weights, *scratch, emit, 8,
    )


def spread(row):
    return jnp.transpose(jnp.broadcast_to(row, (LANES, LANES)))


def target_kernel(
    place, own0, own1, own2, own3, other0, other1, other2, other3, weights, out, *scratch
):
    me = place[0]
    pieces = (own0, own1, own2, own3, other0, other1, other2, other3)

    def emit(at, value):
        for piece in range(value.shape[0] // PART):
            i = (me ^ slot_xor(at // PART + piece)) >> 1
            row = (i & 7) * LANES + (i >> 3) * PART
            out[pl.ds(pl.multiple_of(row, PART), PART), :] = value[piece * PART : (piece + 1) * PART, :]

    graph_layers(
        lambda k: (pieces[k // 4], k % 4),
        lambda k: k ^ slot_of(31),
        lambda link: slot_of(link ^ me),
        weights, *scratch, emit, 16,
    )


def score_kernel(place, own_source, other_source, emb_target, scores, send, e_ref):
    core = place[0] & 1
    e_ref[pl.ds(pl.multiple_of(core * OWN_ROWS, OWN_ROWS), OWN_ROWS), :] = own_source[...]
    e_ref[pl.ds(pl.multiple_of((1 - core) * OWN_ROWS, OWN_ROWS), OWN_ROWS), :] = other_source[...]
    for at in range(0, ROWS, 256):
        rows = pl.ds(at, 256)
        top = None
        for i in range(COL_BLOCKS // 2):
            part = lax.dot_general(
                e_ref[rows, :],
                emb_target[i * 256 : (i + 1) * 256, :],
                (((1,), (1,)), ((), ())),
                preferred_element_type=jnp.float32,
            )
            part = 0.2 * part
            scores[2 * i, rows, :] = part[:, :LANES]
            scores[2 * i + 1, rows, :] = part[:, LANES:]
            larger = jnp.maximum(part[:, :LANES], part[:, LANES:])
            top = larger if top is None else jnp.maximum(top, larger)
        total = jnp.exp(scores[0, rows, :] - top)
        for i in range(1, COL_BLOCKS):
            total += jnp.exp(scores[i, rows, :] - top)
        for half in range(2):
            b = at // LANES + half
            part_top = jnp.transpose(top[half * LANES : (half + 1) * LANES])
            part_total = jnp.transpose(total[half * LANES : (half + 1) * LANES])
            larger = jnp.max(part_top, axis=0, keepdims=True)
            part_total = jnp.sum(part_total * jnp.exp(part_top - larger), axis=0, keepdims=True)
            for d in range(N_ROW_PEERS):
                send[d, b : b + 1, :] = larger
                send[d, ROW_BLOCKS + b : ROW_BLOCKS + b + 1, :] = part_total


def column_kernel(scores, got, weights, tops, send, potential):
    top, total = got[0, 0:ROW_BLOCKS, :], got[0, ROW_BLOCKS:, :]
    larger = top
    for d in range(1, N_ROW_PEERS):
        larger = jnp.maximum(larger, got[d, 0:ROW_BLOCKS, :])
    total = total * jnp.exp(top - larger)
    for d in range(1, N_ROW_PEERS):
        total += got[d, ROW_BLOCKS:, :] * jnp.exp(got[d, 0:ROW_BLOCKS, :] - larger)
    source = LOG_N - (larger + jnp.log(total))
    potential[...] = source
    peaks = [None] * COL_BLOCKS
    for b in range(ROW_BLOCKS):
        rows = pl.ds(b * LANES, LANES)
        shift = spread(source[b : b + 1, :])
        for i in range(COL_BLOCKS):
            x = scores[i, rows, :] + shift
            weights[i, rows, :] = x
            peak = jnp.max(x.reshape(LANES // 8, 8, LANES), axis=0)
            peaks[i] = peak if b == 0 else jnp.maximum(peaks[i], peak)
    step = 64
    for i in range(COL_BLOCKS):
        top = peaks[i]
        total = jnp.zeros((8, LANES), jnp.float32)
        for at in range(0, ROWS, step):
            rows = pl.ds(at, step)
            e = jnp.exp(weights[i, rows, :].reshape(step // 8, 8, LANES) - top[None])
            weights[i, rows, :] = e.reshape(step, LANES)
            total += jnp.sum(e, axis=0)
        tops[i] = top
        larger = jnp.max(top, axis=0, keepdims=True)
        total = jnp.sum(total * jnp.exp(top - larger), axis=0, keepdims=True)
        total = larger + jnp.log(total)
        for d in range(N_PEERS):
            send[d, i : i + 1, :] = total


def row_kernel(weights, tops, got, send, potential, scale):
    larger = got[0]
    for d in range(1, N_PEERS):
        larger = jnp.maximum(larger, got[d])
    total = jnp.exp(got[0] - larger)
    for d in range(1, N_PEERS):
        total += jnp.exp(got[d] - larger)
    target = LOG_N - (larger + jnp.log(total))
    potential[...] = target
    for i in range(COL_BLOCKS):
        scale[i] = jnp.exp(tops[i] + target[i : i + 1, :])
    for b in range(ROW_BLOCKS):
        rows = pl.ds(b * LANES, LANES)
        total = jnp.zeros((LANES // 8, 8, LANES), jnp.float32)
        for i in range(COL_BLOCKS):
            total += weights[i, rows, :].reshape(LANES // 8, 8, LANES) * scale[i][None]
        total = jnp.transpose(total.reshape(LANES, LANES))
        total = jnp.sum(total, axis=0, keepdims=True)
        for d in range(N_ROW_PEERS):
            send[d, b : b + 1, :] = total


def last_kernel(weights, scale, got, before, sums, potential):
    total = got[0]
    for d in range(1, N_ROW_PEERS):
        total += got[d]
    potential[...] = before[...] + (LOG_N - jnp.log(total))
    ratio = 16384.0 / total
    parts = [jnp.zeros((8, LANES), jnp.float32)] * COL_BLOCKS
    for b in range(ROW_BLOCKS):
        rows = pl.ds(b * LANES, LANES)
        factor = spread(ratio[b : b + 1, :])
        for i in range(COL_BLOCKS):
            e = (weights[i, rows, :] * factor).reshape(LANES // 8, 8, LANES)
            parts[i] += jnp.sum(e, axis=0)
    for i in range(COL_BLOCKS):
        total = jnp.sum(parts[i] * scale[i], axis=0, keepdims=True)
        for d in range(N_PEERS):
            sums[d, i : i + 1, :] = total


def call(kernel, outs, scratch, ins, cost=None, limit=VMEM_LIMIT):
    return pl.pallas_call(
        kernel,
        out_shape=[jax.ShapeDtypeStruct(shape, dtype) for shape, dtype in outs],
        in_specs=ins,
        out_specs=[VMEM() for _ in outs],
        scratch_shapes=scratch,
        cost_estimate=cost,
        compiler_params=pltpu.CompilerParams(vmem_limit_bytes=limit),
    )


def graph_scratch(rows):
    return [pltpu.VMEM((rows, D), jnp.bfloat16)] * 3 + [
        pltpu.VMEM((8, LANES), jnp.int32),
        pltpu.SMEM((8, LANES), jnp.int32),
        pltpu.SemaphoreType.DMA,
    ]


def swap(value, axis, size, xor):
    return lax.ppermute(value, axis, [(i, i ^ xor) for i in range(size)])


def direct(value, axis):
    return [value] + [swap(value, axis, 4, xor) for xor in (1, 3, 2)]


def exchange(value, axes):
    return lax.all_to_all(value, axes, 0, 0)


def on_device(
    source_feats, source_tiles, source_links, target_feats, target_tiles, target_links,
    near_first, self_first, near_second, self_second,
):
    f32, bf16 = jnp.float32, jnp.bfloat16
    me = lax.axis_index(("zh", "x", "c"))
    me_source = lax.axis_index(("y", "zl"))

    held, source = pack(target_feats, target_tiles, target_links, source_feats, source_tiles, source_links)
    held, source, *weights = lax.optimization_barrier(
        (held, source, near_first, self_first, near_second, self_second)
    )
    weights = jnp.concatenate(weights, axis=0)
    source = jnp.concatenate([source, swap(source, "zl", 2, 1)], axis=0)
    held = jnp.concatenate(direct(held, "zh"), axis=0)
    held, source, weights = lax.optimization_barrier((held, source, weights))
    source = direct(source, "y")
    own = direct(held, "x")
    source = jnp.concatenate(source, axis=0)
    own[1:], source = lax.optimization_barrier((own[1:], source))
    other = [swap(piece, "c", 2, 1) for piece in own]

    (emb_source,) = call(
        source_kernel,
        [((OWN_ROWS, D), bf16)],
        graph_scratch(OWN_ROWS),
        [SMEM()] + [VMEM()] * 2,
        pl.CostEstimate(flops=700_000_000, bytes_accessed=2_000_000, transcendentals=0),
    )(
        me_source[None],
        source,
        weights,
    )
    other_source = swap(emb_source, "c", 2, 1)

    (emb_target,) = call(
        target_kernel,
        [((COLS, D), bf16)],
        graph_scratch(BLOCK),
        [SMEM()] + [VMEM()] * 9,
        pl.CostEstimate(flops=2_400_000_000, bytes_accessed=4_000_000, transcendentals=0),
    )(me[None], *own, *other, weights)

    emb_target, first = lax.optimization_barrier((emb_target, (me & 1) == 0))
    scores, send = call(
        score_kernel,
        [((COL_BLOCKS, ROWS, LANES), f32), ((N_ROW_PEERS, 2 * ROW_BLOCKS, LANES), f32)],
        [pltpu.VMEM((ROWS, D), bf16)],
        [SMEM()] + [VMEM()] * 3,
    )(me[None], emb_source, other_source, emb_target)

    got = exchange(send, ("c", "y", "zl"))
    spread_weights, tops, send, source_first = call(
        column_kernel,
        [
            ((COL_BLOCKS, ROWS, LANES), f32),
            ((COL_BLOCKS, 8, LANES), f32),
            ((N_PEERS, COL_BLOCKS, LANES), f32),
            ((ROW_BLOCKS, LANES), f32),
        ],
        [],
        [VMEM()] * 2,
    )(scores, got)

    got = exchange(send, ("zh", "x"))
    send, target_first, scale = call(
        row_kernel,
        [((N_ROW_PEERS, ROW_BLOCKS, LANES), f32), ((COL_BLOCKS, LANES), f32), ((COL_BLOCKS, 8, LANES), f32)],
        [],
        [VMEM()] * 3,
    )(spread_weights, tops, got)

    got = exchange(send, ("c", "y", "zl"))
    sums, source_potential = call(
        last_kernel,
        [((N_PEERS, COL_BLOCKS, LANES), f32), ((ROW_BLOCKS, LANES), f32)],
        [],
        [VMEM()] * 4,
    )(spread_weights, scale, got, source_first)

    got = exchange(sums, ("zh", "x"))
    got, first, source_potential, target_first = lax.optimization_barrier(
        (got, first, source_potential, target_first)
    )
    half = target_first + (LOG_N - jnp.log(jnp.sum(got, axis=0)))
    other_half = swap(half, "c", 2, 1)
    even, odd = jnp.where(first, half, other_half), jnp.where(first, other_half, half)
    target_potential = jnp.concatenate(
        [jnp.concatenate([v[:, at : at + PART] for v in (even, odd)], axis=1) for at in (0, PART)], axis=0
    )
    rows = ROW_BLOCKS // 2
    source_potential = jnp.where(first, source_potential[:rows], source_potential[rows:])
    return source_potential.reshape(OWN_ROWS), target_potential.reshape(BLOCK)


def solution(mesh):
    fine = Mesh(mesh.devices.reshape(4, 4, 2, 4, 2), ("zh", "x", "c", "y", "zl"))
    src, tgt = ("zh", "x", "c"), ("y", "zl")
    return jax.shard_map(
        on_device,
        mesh=fine,
        in_specs=(P(src, tgt, None),) * 3 + (P(tgt, src, None),) * 3 + (P(),) * 4,
        out_specs=(P(src), P(tgt)),
        check_vma=False,
    )
```

```python
import functools
import math

import jax
import jax.numpy as jnp
from jax import lax
from jax.experimental import pallas as pl
from jax.experimental.pallas import tpu as pltpu
from jax.sharding import Mesh, PartitionSpec as P

D = 384
PART = 64
PACK = 272
OWN_ROWS = 512
BLOCK = 2048
ROWS = 1024
COLS = 1024
LANES = 128
ROW_BLOCKS = ROWS // LANES
COL_BLOCKS = COLS // LANES
N_ROW_PEERS = 16
STEP = 512
N_PEERS = 16
LOG_N = math.log(16384.0)
VMEM_LIMIT = 18 * 1024 * 1024
PACK_LIMIT = 60 * 1024 * 1024

VMEM = functools.partial(pl.BlockSpec, memory_space=pltpu.VMEM)
HBM = functools.partial(pl.BlockSpec, memory_space=pltpu.HBM)
SMEM = functools.partial(pl.BlockSpec, memory_space=pltpu.SMEM)


def pack_kernel(*refs):
    sources, outs, held, sems = refs[:6], refs[6:8], refs[8:14], refs[14]
    copies = [pltpu.make_async_copy(src, dst, sems.at[i]) for i, (src, dst) in enumerate(zip(sources, held))]
    for copy in copies:
        copy.start()
    for graph, out in enumerate(outs):
        for copy in copies[3 * graph : 3 * graph + 3]:
            copy.wait()
        feats, tiles, links = held[3 * graph : 3 * graph + 3]
        for piece in range(D // LANES):
            out[0, piece * PART : (piece + 1) * PART, :] = feats[0, :, piece * LANES : (piece + 1) * LANES]
        out[0, 3 * PART : 4 * PART, :] = tiles[0]
        link = jnp.broadcast_to(links[0, 0:1, 1:2].astype(jnp.float32), (16, LANES))
        out[0, 4 * PART : PACK, :] = link.astype(jnp.bfloat16)


def pack(*arrays):
    return call(
        pack_kernel,
        [((1, PACK, LANES), jnp.bfloat16)] * 2,
        [pltpu.VMEM(v.shape, v.dtype) for v in arrays] + [pltpu.SemaphoreType.DMA((6,))],
        [HBM()] * 6,
        limit=PACK_LIMIT,
    )(*arrays)


def graph_layers(packed, first, second, weights, x_ref, s_ref, h_ref, emit, wanted):
    count = x_ref.shape[0] // PART
    links = []
    for k in range(count):
        ref, at = packed(k)
        links.append(ref[at, 4 * PART : PACK, :].astype(jnp.float32)[0, 0].astype(jnp.int32))
    for k in range(count):
        ref, at = packed(k)
        for piece in range(D // LANES):
            x_ref[k * PART : (k + 1) * PART, piece * LANES : (piece + 1) * LANES] = ref[
                at, piece * PART : (piece + 1) * PART, :
            ]

    def neighbour_sums(src, count):
        for k in range(count):
            ref, at = packed(k)
            near = src[pl.ds(first(k) * PART, PART), :]
            other = src[pl.ds(pl.multiple_of(second(links[k]) * PART, PART), PART), :]
            panel = ref[at, 3 * PART : 4 * PART, :]
            both = jnp.concatenate([near, other], axis=0)
            total = jnp.dot(panel, both, preferred_element_type=jnp.float32)
            s_ref[k * PART : (k + 1) * PART, :] = total.astype(jnp.bfloat16)

    def mix(src, at, layer):
        left = jnp.concatenate([s_ref[at : at + STEP, :], src[at : at + STEP, :]], axis=1)
        right = weights[layer * 2 * D : (layer + 1) * 2 * D, :]
        return jnp.dot(left, right, preferred_element_type=jnp.float32)

    neighbour_sums(x_ref, count)
    for at in range(0, count * PART, STEP):
        h_ref[at : at + STEP, :] = jnp.maximum(mix(x_ref, at, 0), 0.0).astype(jnp.bfloat16)
    neighbour_sums(h_ref, wanted)
    for at in range(0, wanted * PART, STEP):
        emit(at, mix(h_ref, at, 1).astype(jnp.bfloat16))


def turn(v):
    return v ^ (v >> 1)


def slot_xor(k):
    return (turn(k & 3) << 3) | (turn((k >> 2) & 3) << 1) | (k >> 4)


def slot_of(v):
    return turn(v >> 3) | (turn((v >> 1) & 3) << 2) | ((v & 1) << 4)


def source_xor(k):
    return (turn(k >> 1) << 1) | (k & 1)


source_of = source_xor


def source_kernel(place, packed, weights, out, *scratch):
    me = place[0]

    def emit(at, value):
        for k in range(value.shape[0] // PART):
            q = me ^ source_xor(at // PART + k)
            out[pl.ds(pl.multiple_of(q * PART, PART), PART), :] = value[k * PART : (k + 1) * PART, :]

    graph_layers(
        lambda k: (packed, k),
        lambda k: k ^ source_of(7),
        lambda link: source_of(link ^ me),
        weights, *scratch, emit, 8,
    )


def spread(row):
    return jnp.transpose(jnp.broadcast_to(row, (LANES, LANES)))


def target_kernel(
    place, own_near, own_rest, other_near, other_rest, weights, out, *scratch
):
    me = place[0]
    near, rest = (own_near, other_near), (own_rest, other_rest)

    def emit(at, value):
        for piece in range(value.shape[0] // PART):
            i = (me ^ slot_xor(at // PART + piece)) >> 1
            row = (i & 7) * LANES + (i >> 3) * PART
            out[pl.ds(pl.multiple_of(row, PART), PART), :] = value[piece * PART : (piece + 1) * PART, :]

    graph_layers(
        lambda k: (near[k // 16], k % 16) if k % 16 < 4 else (rest[k // 16], k % 16 - 4),
        lambda k: k ^ slot_of(31),
        lambda link: slot_of(link ^ me),
        weights, *scratch, emit, 16,
    )


def score_kernel(place, own_source, other_source, emb_target, scores, send, e_ref):
    core = place[0] & 1
    e_ref[pl.ds(pl.multiple_of(core * OWN_ROWS, OWN_ROWS), OWN_ROWS), :] = own_source[...]
    e_ref[pl.ds(pl.multiple_of((1 - core) * OWN_ROWS, OWN_ROWS), OWN_ROWS), :] = other_source[...]
    for at in range(0, ROWS, 256):
        rows = pl.ds(at, 256)
        top = None
        for i in range(COL_BLOCKS // 2):
            part = lax.dot_general(
                e_ref[rows, :],
                emb_target[i * 256 : (i + 1) * 256, :],
                (((1,), (1,)), ((), ())),
                preferred_element_type=jnp.float32,
            )
            part = 0.2 * part
            scores[2 * i, rows, :] = part[:, :LANES]
            scores[2 * i + 1, rows, :] = part[:, LANES:]
            larger = jnp.maximum(part[:, :LANES], part[:, LANES:])
            top = larger if top is None else jnp.maximum(top, larger)
        total = jnp.exp(scores[0, rows, :] - top)
        for i in range(1, COL_BLOCKS):
            total += jnp.exp(scores[i, rows, :] - top)
        for half in range(2):
            b = at // LANES + half
            part_top = jnp.transpose(top[half * LANES : (half + 1) * LANES])
            part_total = jnp.transpose(total[half * LANES : (half + 1) * LANES])
            larger = jnp.max(part_top, axis=0, keepdims=True)
            part_total = jnp.sum(part_total * jnp.exp(part_top - larger), axis=0, keepdims=True)
            for d in range(N_ROW_PEERS):
                send[d, b : b + 1, :] = larger
                send[d, ROW_BLOCKS + b : ROW_BLOCKS + b + 1, :] = part_total


def column_kernel(scores, got, weights, tops, send, potential):
    top, total = got[0, 0:ROW_BLOCKS, :], got[0, ROW_BLOCKS:, :]
    larger = top
    for d in range(1, N_ROW_PEERS):
        larger = jnp.maximum(larger, got[d, 0:ROW_BLOCKS, :])
    total = total * jnp.exp(top - larger)
    for d in range(1, N_ROW_PEERS):
        total += got[d, ROW_BLOCKS:, :] * jnp.exp(got[d, 0:ROW_BLOCKS, :] - larger)
    source = LOG_N - (larger + jnp.log(total))
    potential[...] = source
    peaks = [None] * COL_BLOCKS
    for b in range(ROW_BLOCKS):
        rows = pl.ds(b * LANES, LANES)
        shift = spread(source[b : b + 1, :])
        for i in range(COL_BLOCKS):
            x = scores[i, rows, :] + shift
            weights[i, rows, :] = x
            peak = jnp.max(x.reshape(LANES // 8, 8, LANES), axis=0)
            peaks[i] = peak if b == 0 else jnp.maximum(peaks[i], peak)
    step = 64
    for i in range(COL_BLOCKS):
        top = peaks[i]
        total = jnp.zeros((8, LANES), jnp.float32)
        for at in range(0, ROWS, step):
            rows = pl.ds(at, step)
            e = jnp.exp(weights[i, rows, :].reshape(step // 8, 8, LANES) - top[None])
            weights[i, rows, :] = e.reshape(step, LANES)
            total += jnp.sum(e, axis=0)
        tops[i] = top
        larger = jnp.max(top, axis=0, keepdims=True)
        total = jnp.sum(total * jnp.exp(top - larger), axis=0, keepdims=True)
        total = larger + jnp.log(total)
        for d in range(N_PEERS):
            send[d, i : i + 1, :] = total


def row_kernel(weights, tops, got, send, potential, scale):
    larger = got[0]
    for d in range(1, N_PEERS):
        larger = jnp.maximum(larger, got[d])
    total = jnp.exp(got[0] - larger)
    for d in range(1, N_PEERS):
        total += jnp.exp(got[d] - larger)
    target = LOG_N - (larger + jnp.log(total))
    potential[...] = target
    for i in range(COL_BLOCKS):
        scale[i] = jnp.exp(tops[i] + target[i : i + 1, :])
    for b in range(ROW_BLOCKS):
        rows = pl.ds(b * LANES, LANES)
        total = jnp.zeros((LANES // 8, 8, LANES), jnp.float32)
        for i in range(COL_BLOCKS):
            total += weights[i, rows, :].reshape(LANES // 8, 8, LANES) * scale[i][None]
        total = jnp.transpose(total.reshape(LANES, LANES))
        total = jnp.sum(total, axis=0, keepdims=True)
        for d in range(N_ROW_PEERS):
            send[d, b : b + 1, :] = total


def last_kernel(weights, scale, got, before, sums, potential):
    total = got[0]
    for d in range(1, N_ROW_PEERS):
        total += got[d]
    potential[...] = before[...] + (LOG_N - jnp.log(total))
    ratio = 16384.0 / total
    parts = [jnp.zeros((8, LANES), jnp.float32)] * COL_BLOCKS
    for b in range(ROW_BLOCKS):
        rows = pl.ds(b * LANES, LANES)
        factor = spread(ratio[b : b + 1, :])
        for i in range(COL_BLOCKS):
            e = (weights[i, rows, :] * factor).reshape(LANES // 8, 8, LANES)
            parts[i] += jnp.sum(e, axis=0)
    for i in range(COL_BLOCKS):
        total = jnp.sum(parts[i] * scale[i], axis=0, keepdims=True)
        for d in range(N_PEERS):
            sums[d, i : i + 1, :] = total


def call(kernel, outs, scratch, ins, cost=None, limit=VMEM_LIMIT):
    return pl.pallas_call(
        kernel,
        out_shape=[jax.ShapeDtypeStruct(shape, dtype) for shape, dtype in outs],
        in_specs=ins,
        out_specs=[VMEM() for _ in outs],
        scratch_shapes=scratch,
        cost_estimate=cost,
        compiler_params=pltpu.CompilerParams(vmem_limit_bytes=limit),
    )


def graph_scratch(rows):
    return [pltpu.VMEM((rows, D), jnp.bfloat16)] * 3


def swap(value, axis, size, xor):
    return lax.ppermute(value, axis, [(i, i ^ xor) for i in range(size)])


def direct(value, axis):
    return [value] + [swap(value, axis, 4, xor) for xor in (1, 3, 2)]


def exchange(value, axes):
    return lax.all_to_all(value, axes, 0, 0)


def on_device(
    source_feats, source_tiles, source_links, target_feats, target_tiles, target_links,
    near_first, self_first, near_second, self_second,
):
    f32, bf16 = jnp.float32, jnp.bfloat16
    me = lax.axis_index(("zh", "x", "c"))
    me_source = lax.axis_index(("y", "zl"))
    first = (me & 1) == 0

    held, source = pack(target_feats, target_tiles, target_links, source_feats, source_tiles, source_links)
    held, source, me, me_source, first, *weights = lax.optimization_barrier(
        (held, source, me, me_source, first, near_first, self_first, near_second, self_second)
    )
    weights = jnp.concatenate(weights, axis=0)
    source = jnp.concatenate([source, swap(source, "zl", 2, 1)], axis=0)
    held = jnp.concatenate(direct(held, "zh"), axis=0)
    source = jnp.concatenate([source, swap(source, "y", 4, 1)], axis=0)
    held, source, weights = lax.optimization_barrier((held, source, weights))
    source = [source, swap(source, "y", 4, 3)]
    own = direct(held, "x")
    source = jnp.concatenate(source, axis=0)
    own = [own[0], jnp.concatenate(own[1:], axis=0)]
    other_near = swap(own[0], "c", 2, 1)
    own[1], other_near, source = lax.optimization_barrier((own[1], other_near, source))
    other = [other_near, swap(own[1], "c", 2, 1)]

    (emb_source,) = call(
        source_kernel,
        [((OWN_ROWS, D), bf16)],
        graph_scratch(OWN_ROWS),
        [SMEM()] + [VMEM()] * 2,
        pl.CostEstimate(flops=700_000_000, bytes_accessed=2_000_000, transcendentals=0),
    )(
        me_source[None],
        source,
        weights,
    )
    other_source = swap(emb_source, "c", 2, 1)

    (emb_target,) = call(
        target_kernel,
        [((COLS, D), bf16)],
        graph_scratch(BLOCK),
        [SMEM()] + [VMEM()] * 5,
    )(me[None], *own, *other, weights)

    scores, send = call(
        score_kernel,
        [((COL_BLOCKS, ROWS, LANES), f32), ((N_ROW_PEERS, 2 * ROW_BLOCKS, LANES), f32)],
        [pltpu.VMEM((ROWS, D), bf16)],
        [SMEM()] + [VMEM()] * 3,
    )(me[None], emb_source, other_source, emb_target)

    got = exchange(send, ("c", "y", "zl"))
    spread_weights, tops, send, source_first = call(
        column_kernel,
        [
            ((COL_BLOCKS, ROWS, LANES), f32),
            ((COL_BLOCKS, 8, LANES), f32),
            ((N_PEERS, COL_BLOCKS, LANES), f32),
            ((ROW_BLOCKS, LANES), f32),
        ],
        [],
        [VMEM()] * 2,
    )(scores, got)

    got = exchange(send, ("zh", "x"))
    send, target_first, scale = call(
        row_kernel,
        [((N_ROW_PEERS, ROW_BLOCKS, LANES), f32), ((COL_BLOCKS, LANES), f32), ((COL_BLOCKS, 8, LANES), f32)],
        [],
        [VMEM()] * 3,
    )(spread_weights, tops, got)

    got = exchange(send, ("c", "y", "zl"))
    sums, source_potential = call(
        last_kernel,
        [((N_PEERS, COL_BLOCKS, LANES), f32), ((ROW_BLOCKS, LANES), f32)],
        [],
        [VMEM()] * 4,
    )(spread_weights, scale, got, source_first)

    got = exchange(sums, ("zh", "x"))
    got, first, source_potential, target_first = lax.optimization_barrier(
        (got, first, source_potential, target_first)
    )
    half = target_first + (LOG_N - jnp.log(jnp.sum(got, axis=0)))
    other_half = swap(half, "c", 2, 1)
    even, odd = jnp.where(first, half, other_half), jnp.where(first, other_half, half)
    target_potential = jnp.concatenate(
        [jnp.concatenate([v[:, at : at + PART] for v in (even, odd)], axis=1) for at in (0, PART)], axis=0
    )
    rows = ROW_BLOCKS // 2
    source_potential = jnp.where(first, source_potential[:rows], source_potential[rows:])
    return source_potential.reshape(OWN_ROWS), target_potential.reshape(BLOCK)


def solution(mesh):
    fine = Mesh(mesh.devices.reshape(4, 4, 2, 4, 2), ("zh", "x", "c", "y", "zl"))
    src, tgt = ("zh", "x", "c"), ("y", "zl")
    return jax.shard_map(
        on_device,
        mesh=fine,
        in_specs=(P(src, tgt, None),) * 3 + (P(tgt, src, None),) * 3 + (P(),) * 4,
        out_specs=(P(src), P(tgt)),
        check_vma=False,
    )
```

```python
import functools
import math

import jax
import jax.numpy as jnp
from jax import lax
from jax.experimental import pallas as pl
from jax.experimental.pallas import tpu as pltpu
from jax.sharding import Mesh, PartitionSpec as P

D = 384
PART = 64
PACK = 272
OWN_ROWS = 512
BLOCK = 2048
ROWS = 1024
COLS = 1024
LANES = 128
ROW_BLOCKS = ROWS // LANES
COL_BLOCKS = COLS // LANES
N_ROW_PEERS = 16
STEP = 512
N_PEERS = 16
LOG_N = math.log(16384.0)
VMEM_LIMIT = 18 * 1024 * 1024
PACK_LIMIT = 60 * 1024 * 1024

VMEM = functools.partial(pl.BlockSpec, memory_space=pltpu.VMEM)
HBM = functools.partial(pl.BlockSpec, memory_space=pltpu.HBM)
SMEM = functools.partial(pl.BlockSpec, memory_space=pltpu.SMEM)


def pack_kernel(*refs):
    sources, outs, held, sems = refs[:6], refs[6:8], refs[8:14], refs[14]
    copies = [pltpu.make_async_copy(src, dst, sems.at[i]) for i, (src, dst) in enumerate(zip(sources, held))]
    for copy in copies:
        copy.start()
    for graph, out in enumerate(outs):
        for copy in copies[3 * graph : 3 * graph + 3]:
            copy.wait()
        feats, tiles, links = held[3 * graph : 3 * graph + 3]
        for piece in range(D // LANES):
            out[0, piece * PART : (piece + 1) * PART, :] = feats[0, :, piece * LANES : (piece + 1) * LANES]
        out[0, 3 * PART : 4 * PART, :] = tiles[0]
        link = jnp.broadcast_to(links[0, 0:1, 1:2].astype(jnp.float32), (16, LANES))
        out[0, 4 * PART : PACK, :] = link.astype(jnp.bfloat16)


def pack(*arrays):
    return call(
        pack_kernel,
        [((1, PACK, LANES), jnp.bfloat16)] * 2,
        [pltpu.VMEM(v.shape, v.dtype) for v in arrays] + [pltpu.SemaphoreType.DMA((6,))],
        [HBM()] * 6,
        limit=PACK_LIMIT,
    )(*arrays)


def graph_layers(packed, first, second, weights, x_ref, s_ref, h_ref, emit, wanted):
    count = x_ref.shape[0] // PART
    links = []
    for k in range(count):
        ref, at = packed(k)
        links.append(ref[at, 4 * PART : PACK, :].astype(jnp.float32)[0, 0].astype(jnp.int32))
    for k in range(count):
        ref, at = packed(k)
        for piece in range(D // LANES):
            x_ref[k * PART : (k + 1) * PART, piece * LANES : (piece + 1) * LANES] = ref[
                at, piece * PART : (piece + 1) * PART, :
            ]

    def neighbour_sums(src, count):
        for k in range(count):
            ref, at = packed(k)
            near = src[pl.ds(first(k) * PART, PART), :]
            other = src[pl.ds(pl.multiple_of(second(links[k]) * PART, PART), PART), :]
            panel = ref[at, 3 * PART : 4 * PART, :]
            both = jnp.concatenate([near, other], axis=0)
            total = jnp.dot(panel, both, preferred_element_type=jnp.float32)
            s_ref[k * PART : (k + 1) * PART, :] = total.astype(jnp.bfloat16)

    def mix(src, at, layer):
        left = jnp.concatenate([s_ref[at : at + STEP, :], src[at : at + STEP, :]], axis=1)
        right = weights[layer * 2 * D : (layer + 1) * 2 * D, :]
        return jnp.dot(left, right, preferred_element_type=jnp.float32)

    neighbour_sums(x_ref, count)
    for at in range(0, count * PART, STEP):
        h_ref[at : at + STEP, :] = jnp.maximum(mix(x_ref, at, 0), 0.0).astype(jnp.bfloat16)
    neighbour_sums(h_ref, wanted)
    for at in range(0, wanted * PART, STEP):
        emit(at, mix(h_ref, at, 1).astype(jnp.bfloat16))


Z_ORDER = (2, 3, 1)
X_ORDER = (1, 3, 2)


def turn(v, order):
    return ((v & 1) * order[0]) ^ ((v >> 1) * order[1])


def place_of(v, order):
    return turn(v, (order.index(1) + 1, order.index(2) + 1))


def slot_xor(k):
    return (turn(k & 3, Z_ORDER) << 3) | (turn((k >> 2) & 3, X_ORDER) << 1) | (k >> 4)


def slot_of(v):
    return place_of(v >> 3, Z_ORDER) | (place_of((v >> 1) & 3, X_ORDER) << 2) | ((v & 1) << 4)


def source_xor(k):
    return (turn(k >> 1, (1, 3)) << 1) | (k & 1)


source_of = source_xor


def source_kernel(place, packed, weights, out, *scratch):
    me = place[0]

    def emit(at, value):
        for k in range(value.shape[0] // PART):
            q = me ^ source_xor(at // PART + k)
            out[pl.ds(pl.multiple_of(q * PART, PART), PART), :] = value[k * PART : (k + 1) * PART, :]

    graph_layers(
        lambda k: (packed, k),
        lambda k: k ^ source_of(7),
        lambda link: source_of(link ^ me),
        weights, *scratch, emit, 8,
    )


def spread(row):
    return jnp.transpose(jnp.broadcast_to(row, (LANES, LANES)))


def target_kernel(
    place, own_near, own_rest, other_near, other_rest, weights, out, *scratch
):
    me = place[0]
    near, rest = (own_near, other_near), (own_rest, other_rest)

    def emit(at, value):
        for piece in range(value.shape[0] // PART):
            i = (me ^ slot_xor(at // PART + piece)) >> 1
            row = (i & 7) * LANES + (i >> 3) * PART
            out[pl.ds(pl.multiple_of(row, PART), PART), :] = value[piece * PART : (piece + 1) * PART, :]

    graph_layers(
        lambda k: (near[k // 16], k % 16) if k % 16 < 4 else (rest[k // 16], k % 16 - 4),
        lambda k: k ^ slot_of(31),
        lambda link: slot_of(link ^ me),
        weights, *scratch, emit, 16,
    )


def score_kernel(place, own_source, other_source, emb_target, scores, send, e_ref):
    core = place[0] & 1
    e_ref[pl.ds(pl.multiple_of(core * OWN_ROWS, OWN_ROWS), OWN_ROWS), :] = own_source[...]
    e_ref[pl.ds(pl.multiple_of((1 - core) * OWN_ROWS, OWN_ROWS), OWN_ROWS), :] = other_source[...]
    for at in range(0, ROWS, 256):
        rows = pl.ds(at, 256)
        top = None
        for i in range(COL_BLOCKS // 2):
            part = lax.dot_general(
                e_ref[rows, :],
                emb_target[i * 256 : (i + 1) * 256, :],
                (((1,), (1,)), ((), ())),
                preferred_element_type=jnp.float32,
            )
            part = 0.2 * part
            scores[2 * i, rows, :] = part[:, :LANES]
            scores[2 * i + 1, rows, :] = part[:, LANES:]
            larger = jnp.maximum(part[:, :LANES], part[:, LANES:])
            top = larger if top is None else jnp.maximum(top, larger)
        total = jnp.exp(scores[0, rows, :] - top)
        for i in range(1, COL_BLOCKS):
            total += jnp.exp(scores[i, rows, :] - top)
        for half in range(2):
            b = at // LANES + half
            part_top = jnp.transpose(top[half * LANES : (half + 1) * LANES])
            part_total = jnp.transpose(total[half * LANES : (half + 1) * LANES])
            larger = jnp.max(part_top, axis=0, keepdims=True)
            part_total = jnp.sum(part_total * jnp.exp(part_top - larger), axis=0, keepdims=True)
            for d in range(N_ROW_PEERS):
                send[d, b : b + 1, :] = larger
                send[d, ROW_BLOCKS + b : ROW_BLOCKS + b + 1, :] = part_total


def column_kernel(scores, got, weights, tops, send, potential):
    top, total = got[0, 0:ROW_BLOCKS, :], got[0, ROW_BLOCKS:, :]
    larger = top
    for d in range(1, N_ROW_PEERS):
        larger = jnp.maximum(larger, got[d, 0:ROW_BLOCKS, :])
    total = total * jnp.exp(top - larger)
    for d in range(1, N_ROW_PEERS):
        total += got[d, ROW_BLOCKS:, :] * jnp.exp(got[d, 0:ROW_BLOCKS, :] - larger)
    source = LOG_N - (larger + jnp.log(total))
    potential[...] = source
    peaks = [None] * COL_BLOCKS
    for b in range(ROW_BLOCKS):
        rows = pl.ds(b * LANES, LANES)
        shift = spread(source[b : b + 1, :])
        for i in range(COL_BLOCKS):
            x = scores[i, rows, :] + shift
            weights[i, rows, :] = x
            peak = jnp.max(x.reshape(LANES // 8, 8, LANES), axis=0)
            peaks[i] = peak if b == 0 else jnp.maximum(peaks[i], peak)
    step = 64
    for i in range(COL_BLOCKS):
        top = peaks[i]
        total = jnp.zeros((8, LANES), jnp.float32)
        for at in range(0, ROWS, step):
            rows = pl.ds(at, step)
            e = jnp.exp(weights[i, rows, :].reshape(step // 8, 8, LANES) - top[None])
            weights[i, rows, :] = e.reshape(step, LANES)
            total += jnp.sum(e, axis=0)
        tops[i] = top
        larger = jnp.max(top, axis=0, keepdims=True)
        total = jnp.sum(total * jnp.exp(top - larger), axis=0, keepdims=True)
        total = larger + jnp.log(total)
        for d in range(N_PEERS):
            send[d, i : i + 1, :] = total


def row_kernel(weights, tops, got, send, potential, scale):
    larger = got[0]
    for d in range(1, N_PEERS):
        larger = jnp.maximum(larger, got[d])
    total = jnp.exp(got[0] - larger)
    for d in range(1, N_PEERS):
        total += jnp.exp(got[d] - larger)
    target = LOG_N - (larger + jnp.log(total))
    potential[...] = target
    for i in range(COL_BLOCKS):
        scale[i] = jnp.exp(tops[i] + target[i : i + 1, :])
    for b in range(ROW_BLOCKS):
        rows = pl.ds(b * LANES, LANES)
        total = jnp.zeros((LANES // 8, 8, LANES), jnp.float32)
        for i in range(COL_BLOCKS):
            total += weights[i, rows, :].reshape(LANES // 8, 8, LANES) * scale[i][None]
        total = jnp.transpose(total.reshape(LANES, LANES))
        total = jnp.sum(total, axis=0, keepdims=True)
        for d in range(N_ROW_PEERS):
            send[d, b : b + 1, :] = total


def last_kernel(weights, scale, got, before, sums, potential):
    total = got[0]
    for d in range(1, N_ROW_PEERS):
        total += got[d]
    potential[...] = before[...] + (LOG_N - jnp.log(total))
    ratio = 16384.0 / total
    parts = [jnp.zeros((8, LANES), jnp.float32)] * COL_BLOCKS
    for b in range(ROW_BLOCKS):
        rows = pl.ds(b * LANES, LANES)
        factor = spread(ratio[b : b + 1, :])
        for i in range(COL_BLOCKS):
            e = (weights[i, rows, :] * factor).reshape(LANES // 8, 8, LANES)
            parts[i] += jnp.sum(e, axis=0)
    for i in range(COL_BLOCKS):
        total = jnp.sum(parts[i] * scale[i], axis=0, keepdims=True)
        for d in range(N_PEERS):
            sums[d, i : i + 1, :] = total


def call(kernel, outs, scratch, ins, cost=None, limit=VMEM_LIMIT):
    return pl.pallas_call(
        kernel,
        out_shape=[jax.ShapeDtypeStruct(shape, dtype) for shape, dtype in outs],
        in_specs=ins,
        out_specs=[VMEM() for _ in outs],
        scratch_shapes=scratch,
        cost_estimate=cost,
        compiler_params=pltpu.CompilerParams(vmem_limit_bytes=limit),
    )


def graph_scratch(rows):
    return [pltpu.VMEM((rows, D), jnp.bfloat16)] * 3


def swap(value, axis, size, xor):
    return lax.ppermute(value, axis, [(i, i ^ xor) for i in range(size)])


def direct(value, axis, order):
    return [value] + [swap(value, axis, 4, xor) for xor in order]


def exchange(value, axes):
    return lax.all_to_all(value, axes, 0, 0)


def on_device(
    source_feats, source_tiles, source_links, target_feats, target_tiles, target_links,
    near_first, self_first, near_second, self_second,
):
    f32, bf16 = jnp.float32, jnp.bfloat16
    me = lax.axis_index(("zh", "x", "c"))
    me_source = lax.axis_index(("y", "zl"))
    first = (me & 1) == 0

    held, source = pack(target_feats, target_tiles, target_links, source_feats, source_tiles, source_links)
    held, source, me, me_source, first, *weights = lax.optimization_barrier(
        (held, source, me, me_source, first, near_first, self_first, near_second, self_second)
    )
    weights = jnp.concatenate(weights, axis=0)
    source = jnp.concatenate([source, swap(source, "zl", 2, 1)], axis=0)
    held = jnp.concatenate(direct(held, "zh", Z_ORDER), axis=0)
    source = jnp.concatenate([source, swap(source, "y", 4, 1)], axis=0)
    held, source, weights = lax.optimization_barrier((held, source, weights))
    source = [source, swap(source, "y", 4, 3)]
    own = direct(held, "x", X_ORDER)
    source = jnp.concatenate(source, axis=0)
    own = [own[0], jnp.concatenate(own[1:], axis=0)]
    other_near = swap(own[0], "c", 2, 1)

    (emb_source,) = call(
        source_kernel,
        [((OWN_ROWS, D), bf16)],
        graph_scratch(OWN_ROWS),
        [SMEM()] + [VMEM()] * 2,
        pl.CostEstimate(flops=700_000_000, bytes_accessed=2_000_000, transcendentals=0),
    )(
        me_source[None],
        source,
        weights,
    )
    own[1], other_near, emb_source = lax.optimization_barrier((own[1], other_near, emb_source))
    other = [other_near, swap(own[1], "c", 2, 1)]
    other_source = swap(emb_source, "c", 2, 1)

    (emb_target,) = call(
        target_kernel,
        [((COLS, D), bf16)],
        graph_scratch(BLOCK),
        [SMEM()] + [VMEM()] * 5,
    )(me[None], *own, *other, weights)

    scores, send = call(
        score_kernel,
        [((COL_BLOCKS, ROWS, LANES), f32), ((N_ROW_PEERS, 2 * ROW_BLOCKS, LANES), f32)],
        [pltpu.VMEM((ROWS, D), bf16)],
        [SMEM()] + [VMEM()] * 3,
    )(me[None], emb_source, other_source, emb_target)

    got = exchange(send, ("c", "y", "zl"))
    spread_weights, tops, send, source_first = call(
        column_kernel,
        [
            ((COL_BLOCKS, ROWS, LANES), f32),
            ((COL_BLOCKS, 8, LANES), f32),
            ((N_PEERS, COL_BLOCKS, LANES), f32),
            ((ROW_BLOCKS, LANES), f32),
        ],
        [],
        [VMEM()] * 2,
    )(scores, got)

    got = exchange(send, ("zh", "x"))
    send, target_first, scale = call(
        row_kernel,
        [((N_ROW_PEERS, ROW_BLOCKS, LANES), f32), ((COL_BLOCKS, LANES), f32), ((COL_BLOCKS, 8, LANES), f32)],
        [],
        [VMEM()] * 3,
    )(spread_weights, tops, got)

    got = exchange(send, ("c", "y", "zl"))
    sums, source_potential = call(
        last_kernel,
        [((N_PEERS, COL_BLOCKS, LANES), f32), ((ROW_BLOCKS, LANES), f32)],
        [],
        [VMEM()] * 4,
    )(spread_weights, scale, got, source_first)

    got = exchange(sums, ("zh", "x"))
    got, first, source_potential, target_first = lax.optimization_barrier(
        (got, first, source_potential, target_first)
    )
    half = target_first + (LOG_N - jnp.log(jnp.sum(got, axis=0)))
    other_half = swap(half, "c", 2, 1)
    even, odd = jnp.where(first, half, other_half), jnp.where(first, other_half, half)
    target_potential = jnp.concatenate(
        [jnp.concatenate([v[:, at : at + PART] for v in (even, odd)], axis=1) for at in (0, PART)], axis=0
    )
    rows = ROW_BLOCKS // 2
    source_potential = jnp.where(first, source_potential[:rows], source_potential[rows:])
    return source_potential.reshape(OWN_ROWS), target_potential.reshape(BLOCK)


def solution(mesh):
    fine = Mesh(mesh.devices.reshape(4, 4, 2, 4, 2), ("zh", "x", "c", "y", "zl"))
    src, tgt = ("zh", "x", "c"), ("y", "zl")
    return jax.shard_map(
        on_device,
        mesh=fine,
        in_specs=(P(src, tgt, None),) * 3 + (P(tgt, src, None),) * 3 + (P(),) * 4,
        out_specs=(P(src), P(tgt)),
        check_vma=False,
    )
```

```python
import functools
import math

import jax
import jax.numpy as jnp
from jax import lax
from jax.experimental import pallas as pl
from jax.experimental.pallas import tpu as pltpu
from jax.sharding import Mesh, PartitionSpec as P

D = 384
PART = 64
PACK = 272
OWN_ROWS = 512
BLOCK = 2048
ROWS = 1024
COLS = 1024
LANES = 128
ROW_BLOCKS = ROWS // LANES
COL_BLOCKS = COLS // LANES
N_ROW_PEERS = 16
STEP = 512
N_PEERS = 16
LOG_N = math.log(16384.0)
VMEM_LIMIT = 18 * 1024 * 1024
PACK_LIMIT = 60 * 1024 * 1024

VMEM = functools.partial(pl.BlockSpec, memory_space=pltpu.VMEM)
HBM = functools.partial(pl.BlockSpec, memory_space=pltpu.HBM)
SMEM = functools.partial(pl.BlockSpec, memory_space=pltpu.SMEM)


def pack_kernel(*refs):
    sources, outs, held, sems = refs[:6], refs[6:8], refs[8:14], refs[14]
    copies = [pltpu.make_async_copy(src, dst, sems.at[i]) for i, (src, dst) in enumerate(zip(sources, held))]
    for copy in copies:
        copy.start()
    for graph, out in enumerate(outs):
        for copy in copies[3 * graph : 3 * graph + 3]:
            copy.wait()
        feats, tiles, links = held[3 * graph : 3 * graph + 3]
        for piece in range(D // LANES):
            out[0, piece * PART : (piece + 1) * PART, :] = feats[0, :, piece * LANES : (piece + 1) * LANES]
        out[0, 3 * PART : 4 * PART, :] = tiles[0]
        link = jnp.broadcast_to(links[0, 0:1, 1:2].astype(jnp.float32), (16, LANES))
        out[0, 4 * PART : PACK, :] = link.astype(jnp.bfloat16)


def pack(*arrays):
    return call(
        pack_kernel,
        [((1, PACK, LANES), jnp.bfloat16)] * 2,
        [pltpu.VMEM(v.shape, v.dtype) for v in arrays] + [pltpu.SemaphoreType.DMA((6,))],
        [HBM()] * 6,
        limit=PACK_LIMIT,
    )(*arrays)


def graph_layers(packed, first, second, weights, x_ref, s_ref, h_ref, emit, wanted):
    count = x_ref.shape[0] // PART
    links = []
    for k in range(count):
        ref, at = packed(k)
        links.append(ref[at, 4 * PART : PACK, :].astype(jnp.float32)[0, 0].astype(jnp.int32))
    for k in range(count):
        ref, at = packed(k)
        for piece in range(D // LANES):
            x_ref[k * PART : (k + 1) * PART, piece * LANES : (piece + 1) * LANES] = ref[
                at, piece * PART : (piece + 1) * PART, :
            ]

    def neighbour_sums(src, count):
        for k in range(count):
            ref, at = packed(k)
            near = src[pl.ds(first(k) * PART, PART), :]
            other = src[pl.ds(pl.multiple_of(second(links[k]) * PART, PART), PART), :]
            panel = ref[at, 3 * PART : 4 * PART, :]
            both = jnp.concatenate([near, other], axis=0)
            total = jnp.dot(panel, both, preferred_element_type=jnp.float32)
            s_ref[k * PART : (k + 1) * PART, :] = total.astype(jnp.bfloat16)

    def mix(src, at, layer):
        left = jnp.concatenate([s_ref[at : at + STEP, :], src[at : at + STEP, :]], axis=1)
        right = weights[layer * 2 * D : (layer + 1) * 2 * D, :]
        return jnp.dot(left, right, preferred_element_type=jnp.float32)

    neighbour_sums(x_ref, count)
    for at in range(0, count * PART, STEP):
        h_ref[at : at + STEP, :] = jnp.maximum(mix(x_ref, at, 0), 0.0).astype(jnp.bfloat16)
    neighbour_sums(h_ref, wanted)
    for at in range(0, wanted * PART, STEP):
        emit(at, mix(h_ref, at, 1).astype(jnp.bfloat16))


Z_ORDER = (2, 3, 1)
X_ORDER = (1, 3, 2)


def turn(v, order):
    return ((v & 1) * order[0]) ^ ((v >> 1) * order[1])


def place_of(v, order):
    return turn(v, (order.index(1) + 1, order.index(2) + 1))


def slot_xor(k):
    return (turn(k & 3, Z_ORDER) << 3) | (turn((k >> 2) & 3, X_ORDER) << 1) | (k >> 4)


def slot_of(v):
    return place_of(v >> 3, Z_ORDER) | (place_of((v >> 1) & 3, X_ORDER) << 2) | ((v & 1) << 4)


def source_xor(k):
    return (turn(k >> 1, (1, 3)) << 1) | (k & 1)


source_of = source_xor


def source_kernel(place, packed, weights, out, *scratch):
    me = place[0]

    def emit(at, value):
        for k in range(value.shape[0] // PART):
            q = me ^ source_xor(at // PART + k)
            out[pl.ds(pl.multiple_of(q * PART, PART), PART), :] = value[k * PART : (k + 1) * PART, :]

    graph_layers(
        lambda k: (packed, k),
        lambda k: k ^ source_of(7),
        lambda link: source_of(link ^ me),
        weights, *scratch, emit, 8,
    )


def spread(row):
    return jnp.transpose(jnp.broadcast_to(row, (LANES, LANES)))


def target_kernel(
    place, own_near, own_rest, other_near, other_rest, weights, out, *scratch
):
    me = place[0]
    near, rest = (own_near, other_near), (own_rest, other_rest)

    def emit(at, value):
        for piece in range(value.shape[0] // PART):
            i = (me ^ slot_xor(at // PART + piece)) >> 1
            row = (i & 7) * LANES + (i >> 3) * PART
            out[pl.ds(pl.multiple_of(row, PART), PART), :] = value[piece * PART : (piece + 1) * PART, :]

    graph_layers(
        lambda k: (near[k // 16], k % 16) if k % 16 < 4 else (rest[k // 16], k % 16 - 4),
        lambda k: k ^ slot_of(31),
        lambda link: slot_of(link ^ me),
        weights, *scratch, emit, 16,
    )


def score_kernel(own_source, other_source, emb_target, scores, send):
    for at in range(0, ROWS, 256):
        rows = pl.ds(at, 256)
        half_ref, start = (own_source, at) if at < OWN_ROWS else (other_source, at - OWN_ROWS)
        top = None
        for i in range(COL_BLOCKS // 2):
            part = lax.dot_general(
                half_ref[start : start + 256, :],
                emb_target[i * 256 : (i + 1) * 256, :],
                (((1,), (1,)), ((), ())),
                preferred_element_type=jnp.float32,
            )
            part = 0.2 * part
            scores[2 * i, rows, :] = part[:, :LANES]
            scores[2 * i + 1, rows, :] = part[:, LANES:]
            larger = jnp.maximum(part[:, :LANES], part[:, LANES:])
            top = larger if top is None else jnp.maximum(top, larger)
        total = jnp.exp(scores[0, rows, :] - top)
        for i in range(1, COL_BLOCKS):
            total += jnp.exp(scores[i, rows, :] - top)
        for half in range(2):
            b = at // LANES + half
            part_top = jnp.transpose(top[half * LANES : (half + 1) * LANES])
            part_total = jnp.transpose(total[half * LANES : (half + 1) * LANES])
            larger = jnp.max(part_top, axis=0, keepdims=True)
            part_total = jnp.sum(part_total * jnp.exp(part_top - larger), axis=0, keepdims=True)
            for d in range(N_ROW_PEERS):
                send[d, b : b + 1, :] = larger
                send[d, ROW_BLOCKS + b : ROW_BLOCKS + b + 1, :] = part_total


def own_first(place, low, high):
    same = place[0] & 1 == 0
    mine, theirs = jnp.where(same, low, high), jnp.where(same, high, low)
    half = ROW_BLOCKS // 2
    return mine, jnp.concatenate([theirs[half:], theirs[:half]], axis=0)


def column_kernel(place, scores, got, weights, tops, send, potential):
    tops_of, totals_of = [], []
    for start in (0, N_ROW_PEERS // 2):
        peers = range(start, start + N_ROW_PEERS // 2)
        larger = got[start, 0:ROW_BLOCKS, :]
        for d in peers[1:]:
            larger = jnp.maximum(larger, got[d, 0:ROW_BLOCKS, :])
        total = jnp.zeros((ROW_BLOCKS, LANES), jnp.float32)
        for d in peers:
            total += got[d, ROW_BLOCKS:, :] * jnp.exp(got[d, 0:ROW_BLOCKS, :] - larger)
        tops_of.append(larger)
        totals_of.append(total)
    tops_of, totals_of = own_first(place, *tops_of), own_first(place, *totals_of)
    larger = jnp.maximum(*tops_of)
    total = sum(part * jnp.exp(top - larger) for part, top in zip(totals_of, tops_of))
    source = LOG_N - (larger + jnp.log(total))
    potential[...] = source
    peaks = [None] * COL_BLOCKS
    for b in range(ROW_BLOCKS):
        rows = pl.ds(b * LANES, LANES)
        shift = spread(source[b : b + 1, :])
        for i in range(COL_BLOCKS):
            x = scores[i, rows, :] + shift
            weights[i, rows, :] = x
            peak = jnp.max(x.reshape(LANES // 8, 8, LANES), axis=0)
            peaks[i] = peak if b == 0 else jnp.maximum(peaks[i], peak)
    step = 64
    for i in range(COL_BLOCKS):
        top = peaks[i]
        total = jnp.zeros((8, LANES), jnp.float32)
        for at in range(0, ROWS, step):
            rows = pl.ds(at, step)
            e = jnp.exp(weights[i, rows, :].reshape(step // 8, 8, LANES) - top[None])
            weights[i, rows, :] = e.reshape(step, LANES)
            total += jnp.sum(e, axis=0)
        tops[i] = top
        larger = jnp.max(top, axis=0, keepdims=True)
        total = jnp.sum(total * jnp.exp(top - larger), axis=0, keepdims=True)
        total = larger + jnp.log(total)
        for d in range(N_PEERS):
            send[d, i : i + 1, :] = total


def row_kernel(weights, tops, got, send, potential, scale):
    larger = got[0]
    for d in range(1, N_PEERS):
        larger = jnp.maximum(larger, got[d])
    total = jnp.exp(got[0] - larger)
    for d in range(1, N_PEERS):
        total += jnp.exp(got[d] - larger)
    target = LOG_N - (larger + jnp.log(total))
    potential[...] = target
    for i in range(COL_BLOCKS):
        scale[i] = jnp.exp(tops[i] + target[i : i + 1, :])
    for b in range(ROW_BLOCKS):
        rows = pl.ds(b * LANES, LANES)
        total = jnp.zeros((LANES // 8, 8, LANES), jnp.float32)
        for i in range(COL_BLOCKS):
            total += weights[i, rows, :].reshape(LANES // 8, 8, LANES) * scale[i][None]
        total = jnp.transpose(total.reshape(LANES, LANES))
        total = jnp.sum(total, axis=0, keepdims=True)
        for d in range(N_ROW_PEERS):
            send[d, b : b + 1, :] = total


def last_kernel(place, weights, scale, got, before, sums, potential):
    parts = []
    for start in (0, N_ROW_PEERS // 2):
        total = got[start]
        for d in range(start + 1, start + N_ROW_PEERS // 2):
            total += got[d]
        parts.append(total)
    total = sum(own_first(place, *parts))
    potential[...] = before[...] + (LOG_N - jnp.log(total))
    ratio = 16384.0 / total
    parts = [jnp.zeros((8, LANES), jnp.float32)] * COL_BLOCKS
    for b in range(ROW_BLOCKS):
        rows = pl.ds(b * LANES, LANES)
        factor = spread(ratio[b : b + 1, :])
        for i in range(COL_BLOCKS):
            e = (weights[i, rows, :] * factor).reshape(LANES // 8, 8, LANES)
            parts[i] += jnp.sum(e, axis=0)
    for i in range(COL_BLOCKS):
        total = jnp.sum(parts[i] * scale[i], axis=0, keepdims=True)
        for d in range(N_PEERS):
            sums[d, i : i + 1, :] = total


def call(kernel, outs, scratch, ins, cost=None, limit=VMEM_LIMIT):
    return pl.pallas_call(
        kernel,
        out_shape=[jax.ShapeDtypeStruct(shape, dtype) for shape, dtype in outs],
        in_specs=ins,
        out_specs=[VMEM() for _ in outs],
        scratch_shapes=scratch,
        cost_estimate=cost,
        compiler_params=pltpu.CompilerParams(vmem_limit_bytes=limit),
    )


def graph_scratch(rows):
    return [pltpu.VMEM((rows, D), jnp.bfloat16)] * 3


def swap(value, axis, size, xor):
    return lax.ppermute(value, axis, [(i, i ^ xor) for i in range(size)])


def direct(value, axis, order):
    return [value] + [swap(value, axis, 4, xor) for xor in order]


def exchange(value, axes):
    return lax.all_to_all(value, axes, 0, 0)


def on_device(
    source_feats, source_tiles, source_links, target_feats, target_tiles, target_links,
    near_first, self_first, near_second, self_second,
):
    f32, bf16 = jnp.float32, jnp.bfloat16
    me = lax.axis_index(("zh", "x", "c"))
    me_source = lax.axis_index(("y", "zl"))
    first = (me & 1) == 0

    held, source = pack(target_feats, target_tiles, target_links, source_feats, source_tiles, source_links)
    held, source, me, me_source, first, *weights = lax.optimization_barrier(
        (held, source, me, me_source, first, near_first, self_first, near_second, self_second)
    )
    weights = jnp.concatenate(weights, axis=0)
    source = jnp.concatenate([source, swap(source, "zl", 2, 1)], axis=0)
    held = jnp.concatenate(direct(held, "zh", Z_ORDER), axis=0)
    source = jnp.concatenate([source, swap(source, "y", 4, 1)], axis=0)
    held, source, weights = lax.optimization_barrier((held, source, weights))
    source = [source, swap(source, "y", 4, 3)]
    own = direct(held, "x", X_ORDER)
    source = jnp.concatenate(source, axis=0)
    own = [own[0], jnp.concatenate(own[1:], axis=0)]
    other_near = swap(own[0], "c", 2, 1)

    (emb_source,) = call(
        source_kernel,
        [((OWN_ROWS, D), bf16)],
        graph_scratch(OWN_ROWS),
        [SMEM()] + [VMEM()] * 2,
        pl.CostEstimate(flops=700_000_000, bytes_accessed=2_000_000, transcendentals=0),
    )(
        me_source[None],
        source,
        weights,
    )
    own[1], other_near, emb_source = lax.optimization_barrier((own[1], other_near, emb_source))
    other = [other_near, swap(own[1], "c", 2, 1)]
    other_source = swap(emb_source, "c", 2, 1)

    (emb_target,) = call(
        target_kernel,
        [((COLS, D), bf16)],
        graph_scratch(BLOCK),
        [SMEM()] + [VMEM()] * 5,
    )(me[None], *own, *other, weights)

    scores, send = call(
        score_kernel,
        [((COL_BLOCKS, ROWS, LANES), f32), ((N_ROW_PEERS, 2 * ROW_BLOCKS, LANES), f32)],
        [],
        [VMEM()] * 3,
    )(emb_source, other_source, emb_target)

    got = exchange(send, ("c", "y", "zl"))
    spread_weights, tops, send, source_first = call(
        column_kernel,
        [
            ((COL_BLOCKS, ROWS, LANES), f32),
            ((COL_BLOCKS, 8, LANES), f32),
            ((N_PEERS, COL_BLOCKS, LANES), f32),
            ((ROW_BLOCKS, LANES), f32),
        ],
        [],
        [SMEM()] + [VMEM()] * 2,
    )(me[None], scores, got)

    got = exchange(send, ("zh", "x"))
    send, target_first, scale = call(
        row_kernel,
        [((N_ROW_PEERS, ROW_BLOCKS, LANES), f32), ((COL_BLOCKS, LANES), f32), ((COL_BLOCKS, 8, LANES), f32)],
        [],
        [VMEM()] * 3,
    )(spread_weights, tops, got)

    got = exchange(send, ("c", "y", "zl"))
    sums, source_potential = call(
        last_kernel,
        [((N_PEERS, COL_BLOCKS, LANES), f32), ((ROW_BLOCKS, LANES), f32)],
        [],
        [SMEM()] + [VMEM()] * 4,
    )(me[None], spread_weights, scale, got, source_first)

    got = exchange(sums, ("zh", "x"))
    got, first, source_potential, target_first = lax.optimization_barrier(
        (got, first, source_potential, target_first)
    )
    half = target_first + (LOG_N - jnp.log(jnp.sum(got, axis=0)))
    other_half = swap(half, "c", 2, 1)
    even, odd = jnp.where(first, half, other_half), jnp.where(first, other_half, half)
    target_potential = jnp.concatenate(
        [jnp.concatenate([v[:, at : at + PART] for v in (even, odd)], axis=1) for at in (0, PART)], axis=0
    )
    rows = ROW_BLOCKS // 2
    return source_potential[:rows].reshape(OWN_ROWS), target_potential.reshape(BLOCK)


def solution(mesh):
    fine = Mesh(mesh.devices.reshape(4, 4, 2, 4, 2), ("zh", "x", "c", "y", "zl"))
    src, tgt = ("zh", "x", "c"), ("y", "zl")
    return jax.shard_map(
        on_device,
        mesh=fine,
        in_specs=(P(src, tgt, None),) * 3 + (P(tgt, src, None),) * 3 + (P(),) * 4,
        out_specs=(P(src), P(tgt)),
        check_vma=False,
    )
```
